32 devices in a mesh: src: 8 (over z, x), rcv: 4 (over y, core).
Axes of the slice: x: 2, y: 2, z: 4, core: 2. Of those that a mesh axis runs over, the one named last changes fastest.
Arguments:
- probes: bfloat16 [256, 128, 256], P('rcv', 'src'), may hold values from -6 to 6
- kappa: float32 [128, 256], P('src'), may hold values from 0.02 to 0.24
- footprint: bfloat16 [8, 4, 192, 128, 128], P('src', 'rcv'), may hold values from -0.109375 to 0.109375
- block_source: int32 [8, 4, 192], P('src', 'rcv'), may hold values from 0 to 31
- block_receptor: int32 [8, 4, 192], P('src', 'rcv'), may hold values from 0 to 15
- block_count: int32 [8, 4], P('src', 'rcv'), may hold values from 1 to 192, as said below
- obs_weight: float32 [8192], P('rcv'), may hold values from 1 to 8
Outputs:
- hessian_probe: float32 [256, 128, 256], P('rcv', 'src')
The draws below stay inside these ranges and needn't reach their ends.
Inputs may be any that keep to these rules, and one draw needn't show every extreme that they name: Slots 0 to block_count - 1 of a tile and group hold its footprint blocks, later slots are unused; some tile and group uses all 192 slots.
All inputs are finite; a program needn't handle non-finite values.
Results may differ from the reference program's by a relative error of at most 0.006.
Values may be sent and summed in bfloat16 or wider, within the bound.
No kernel may reach another device: no remote copies, remote signals or barrier semaphores. Data moves between devices by JAX's collectives and lax.ppermute only.
A program may use at most 64 MiB of HBM per device.

```python
import math
import jax
import jax.numpy as jnp
from jax import lax

BLK = 128
NLON = 256
RB_LOC = 16
NB = 192
SMOOTH = 4
SB = 32
NLAT = 128
P_SIZE = 256
NREC = 8192
N_SRC = 8
N_RCV = 4


def draw_block_count(key, part):
    first_key, second_key, third_key = jax.random.split(key, 3)
    factor_one = jax.random.randint(first_key, (N_SRC, N_RCV), 0, NB)
    factor_two = jax.random.randint(second_key, (N_SRC, N_RCV), 0, NB)
    counts = factor_one * factor_two // NB + 1
    busiest = jax.random.randint(third_key, (), 0, N_SRC * N_RCV)
    flat_counts = jnp.where(jnp.arange(N_SRC * N_RCV) == busiest, NB, counts.reshape(-1))
    return flat_counts.reshape(N_SRC, N_RCV).astype(jnp.int32)


def touch_ends(drawn, own_key, smallest, largest):
    index_at = [jax.random.randint(jax.random.fold_in(own_key, axis), (), 0, length) for axis, length in enumerate(drawn.shape)]
    longest = drawn.shape.index(max(drawn.shape))
    neighbour = index_at[:longest] + [(index_at[longest] + 1) % drawn.shape[longest]] + index_at[longest + 1:]
    return drawn.at[tuple(index_at)].set(smallest).at[tuple(neighbour)].set(largest)


def shard_levels(rng, shape, shards, low, high):
    level, own = 1.0, jax.random.fold_in(rng, 6)
    for position, blocks in shards:
        heights = jnp.exp(jax.random.uniform(jax.random.fold_in(own, position), (blocks,), jnp.float32, low / len(shards), high / len(shards)))
        level = level * jnp.repeat(heights, shape[position] // blocks).reshape([-1 if axis == position else 1 for axis in range(len(shape))])
    return level


def centred(key, shape, spread, limit, cuts=(), kind=jnp.bfloat16):
    gain = shard_levels(key, shape, cuts, -0.22, 0.18) if cuts else 1.0
    entries = jax.random.normal(key, shape, jnp.float32) * spread * gain
    return jnp.minimum(jnp.maximum(entries, -limit), limit).astype(kind)


def setup_inputs(seed: int = 0) -> dict:
    key_list = jax.random.split(jax.random.key(seed), 8)
    probes = centred(key_list[0], (P_SIZE, NLAT, NLON), 1.0, 6.0, ((0, 4), (1, 8)))
    kappa = jnp.clip(jnp.exp(math.log(0.24) - 2.4849066 * jax.random.uniform(key_list[1], (NLAT, NLON), jnp.float32) ** shard_levels(key_list[1], (NLAT, NLON), ((0, 8),), -0.2, 0.2)), 0.02, 0.24)
    footprint = centred(key_list[2], (N_SRC, N_RCV, NB, BLK, BLK), (N_SRC * NB * BLK // (4 * RB_LOC)) ** -0.5, 0.109375, ((0, 8), (1, 4)))
    block_source = touch_ends(jax.random.randint(key_list[3], (N_SRC, N_RCV, NB), 0, SB), jax.random.fold_in(key_list[3], 1), 0, SB - 1).astype(jnp.int32)
    block_receptor = touch_ends(jax.random.randint(key_list[4], (N_SRC, N_RCV, NB), 0, RB_LOC), jax.random.fold_in(key_list[4], 1), 0, RB_LOC - 1).astype(jnp.int32)
    block_count = draw_block_count(jax.random.fold_in(key_list[7], 71), 0)
    obs_weight = jnp.clip(jnp.exp(math.log(8.0) - 2.0794415 * jax.random.uniform(key_list[6], (NREC,), jnp.float32) ** shard_levels(key_list[6], (NREC,), ((0, 4),), -0.2, 0.2)), 1.0, 8.0)
    return {"probes": probes, "kappa": kappa, "footprint": footprint, "block_source": block_source, "block_receptor": block_receptor, "block_count": block_count, "obs_weight": obs_weight}


def laplacian_operator(emission_source_field):
    padded = jnp.pad(emission_source_field, ((0, 0), (1, 1), (1, 1)))
    return padded[:, 2:, 1:-1] + padded[:, :-2, 1:-1] + padded[:, 1:-1, 2:] + padded[:, 1:-1, :-2] - 4.0 * emission_source_field


def device_forward(blocks, sources, receptors, used_slots, tile_field):
    selected_entries = jnp.take(tile_field, sources, axis=0).astype(jnp.float32)
    hessian_result = jnp.einsum("nrc,ncp->nrp", blocks.astype(jnp.float32), selected_entries)
    in_use = jnp.arange(blocks.shape[0], dtype=jnp.int32) < used_slots
    onehot = ((receptors[:, None] == jnp.arange(RB_LOC, dtype=jnp.int32)[None, :]) & in_use[:, None]).astype(jnp.float32)
    return jnp.einsum("nrp,nb->brp", hessian_result, onehot, precision=lax.Precision.HIGHEST)


def device_adjoint(blocks, sources, receptors, used_slots, weighted_group):
    selected_entries = jnp.take(weighted_group, receptors, axis=0).astype(jnp.float32)
    hessian_result = jnp.einsum("nrc,nrp->ncp", blocks.astype(jnp.float32), selected_entries)
    in_use = jnp.arange(blocks.shape[0], dtype=jnp.int32) < used_slots
    onehot = ((sources[:, None] == jnp.arange(SB, dtype=jnp.int32)[None, :]) & in_use[:, None]).astype(jnp.float32)
    return jnp.einsum("ncp,ns->scp", hessian_result, onehot, precision=lax.Precision.HIGHEST)


def reference(probes, kappa, footprint, block_source, block_receptor, block_count, obs_weight):
    smoothed = probes.astype(jnp.float32)
    for repeat in range(SMOOTH):
        smoothed = smoothed + kappa * laplacian_operator(smoothed)
    truncated_field = lax.optimization_barrier(smoothed.astype(jnp.bfloat16))
    tile_fields = truncated_field.reshape(P_SIZE, N_SRC, SB, BLK).transpose(1, 2, 3, 0)

    def forward_tile(running, inputs):
        blocks, sources, receptors, counts, tile_field = inputs
        block_terms = jax.vmap(device_forward, in_axes=(0, 0, 0, 0, None))(blocks, sources, receptors, counts, tile_field)
        return running + block_terms, None

    initial = jnp.zeros((N_RCV, RB_LOC, BLK, P_SIZE), jnp.float32)
    evolved, unused = lax.scan(forward_tile, initial, (footprint, block_source, block_receptor, block_count, tile_fields))
    weighted = lax.optimization_barrier((obs_weight.reshape(N_RCV, RB_LOC, BLK, 1) * evolved).astype(jnp.bfloat16))

    def adjoint_tile(running, inputs):
        blocks, sources, receptors, counts = inputs
        block_terms = jax.vmap(device_adjoint)(blocks, sources, receptors, counts, weighted)
        rounded = lax.optimization_barrier(block_terms.astype(jnp.bfloat16))
        return running, jnp.sum(rounded.astype(jnp.float32), axis=0)

    dummy = jnp.zeros((), jnp.float32)
    dummy, adjoint_pass = lax.scan(adjoint_tile, dummy, (footprint, block_source, block_receptor, block_count))
    adjoint_pass = adjoint_pass.transpose(3, 0, 1, 2).reshape(P_SIZE, NLAT, NLON)
    back = adjoint_pass
    for repeat in range(SMOOTH):
        back = back + laplacian_operator(kappa * back)
    return probes.astype(jnp.float32) + back
```

```python
import jax
import jax.numpy as jnp
from jax import lax
from jax.experimental import pallas as pl
from jax.experimental.pallas import tpu as pltpu
from jax.sharding import PartitionSpec as P

BLK = 128
RB_LOC = 16
SMOOTH = 4
SUB = 8
PIECES = 16
GROUP = 32
F32, BF16 = jnp.float32, jnp.bfloat16
VMEM = pl.BlockSpec(memory_space=pltpu.VMEM)
SMEM = pl.BlockSpec(memory_space=pltpu.SMEM)


def params(mib=32):
    return pltpu.CompilerParams(vmem_limit_bytes=mib * 1024 * 1024)


def widen(probes_ref, wide):
    for h in range(wide.shape[0]):
        wide[h] = probes_ref[:, h * BLK : (h + 1) * BLK].astype(F32)


def one_row(wide, start, size, rows):
    at = pl.ds(start, size, stride=rows)
    return jnp.concatenate([wide[h, at, :] for h in range(wide.shape[0])], axis=1)


def edge_kernel(probes_ref, kappa_ref, north_ref, south_ref, wide):
    rows, lon = kappa_ref.shape
    probe_local = probes_ref.shape[0] // rows
    widen(probes_ref, wide)
    place = lax.broadcasted_iota(jnp.int32, (PIECES, lon), 0)
    for out_ref, first in ((north_ref, 0), (south_ref, rows - SMOOTH)):
        for r in range(SMOOTH):
            out_ref[r, :probe_local, :] = one_row(wide, first + r, probe_local, rows).astype(BF16)
            whole = kappa_ref[first + r : first + r + 1, :]
            high = whole.astype(BF16).astype(F32)
            rest = whole - high
            middle = rest.astype(BF16).astype(F32)
            low = rest - middle
            pieces = jnp.where(place == 0, high, jnp.where(place == 1, middle, jnp.where(place == 2, low, 0.0)))
            out_ref[r, probe_local:, :] = pieces.astype(BF16)


def kappa_rows(kappa_ref, above_ref, below_ref, probe_local):
    def halo(ref, r):
        piece = ref[r, probe_local:, :].astype(F32)
        return piece[0:1] + piece[1:2] + piece[2:3]

    rows = kappa_ref.shape[0]
    return (
        [halo(above_ref, r) for r in range(SMOOTH)]
        + [kappa_ref[r : r + 1, :] for r in range(rows)]
        + [halo(below_ref, r) for r in range(SMOOTH)]
    )


def smooth_kernel(probes_ref, kappa_ref, above_ref, below_ref, field_ref, wide, coef, halos, result):
    rows, lon = kappa_ref.shape
    probe_local = probes_ref.shape[0] // rows
    total = rows + 2 * SMOOTH
    widen(probes_ref, wide)
    halos[0] = above_ref[:, :probe_local, :].astype(F32)
    halos[1] = below_ref[:, :probe_local, :].astype(F32)
    lane = lax.broadcasted_iota(jnp.int32, (SUB, lon), 1)
    for r, k in enumerate(kappa_rows(kappa_ref, above_ref, below_ref, probe_local)):
        k = jnp.broadcast_to(k, (SUB, lon))
        coef[0, r] = k
        coef[1, r] = jnp.where(lane > 0, k, 0.0)
        coef[2, r] = jnp.where(lane < lon - 1, k, 0.0)

    @pl.loop(0, probe_local // SUB)
    def _(c):
        base = pl.multiple_of(c * SUB, SUB)
        f = (
            [halos[0, r, pl.ds(base, SUB), :] for r in range(SMOOTH)]
            + [one_row(wide, base * rows + r, SUB, rows) for r in range(rows)]
            + [halos[1, r, pl.ds(base, SUB), :] for r in range(SMOOTH)]
        )
        for step in range(SMOOTH):
            new = list(f)
            for r in range(step + 1, total - step - 1):
                k, kl, kr = coef[0, r], coef[1, r], coef[2, r]
                g = f[r]
                new[r] = (
                    g
                    + k * (f[r - 1] + f[r + 1] - 4.0 * g)
                    + kl * pltpu.roll(g, 1, 1)
                    + kr * pltpu.roll(g, lon - 1, 1)
                )
            f = new
        for r in range(rows):
            for h in range(lon // BLK):
                result[r * (lon // BLK) + h, pl.ds(base, SUB), :] = f[r + SMOOTH][:, h * BLK : (h + 1) * BLK]

    field_ref[...] = result[...].astype(BF16)


def forward_kernel(sources, receptors, count, blocks_ref, near_ref, far_ref, out_ref, total):
    g = pl.program_id(0)

    @pl.when(g == 0)
    def _():
        total[...] = jnp.zeros_like(total)

    group = blocks_ref.shape[0]
    spare = total.shape[0] - 1
    for i in range(group):
        n = g * group + i
        j = sources[n]
        b = jnp.where(n < count[0], receptors[n], spare)
        entries = jnp.concatenate([near_ref[j], far_ref[j]], axis=0)
        total[b] += lax.dot_general(
            entries, blocks_ref[i], (((1,), (1,)), ((), ())), preferred_element_type=F32
        )

    @pl.when(g == pl.num_programs(0) - 1)
    def _():
        out_ref[...] = total[:spare].astype(BF16)


def adjoint_kernel(sources, receptors, count, blocks_ref, weighted_ref, near_ref, far_ref, total):
    g = pl.program_id(0)

    @pl.when(g == 0)
    def _():
        total[...] = jnp.zeros_like(total)

    group = blocks_ref.shape[0]
    spare = total.shape[0] - 1
    for i in range(group):
        n = g * group + i
        j = jnp.where(n < count[0], sources[n], spare)
        total[j] += jnp.dot(weighted_ref[receptors[n]], blocks_ref[i], preferred_element_type=F32)

    @pl.when(g == pl.num_programs(0) - 1)
    def _():
        half = near_ref.shape[1]
        near_ref[...] = total[:spare, :half].astype(BF16)
        far_ref[...] = total[:spare, half:].astype(BF16)


def back_kernel(
    inside, probes_ref, kappa_ref, above_ref, below_ref, own_ref, core_ref, far_ref, top_ref, bottom_ref, out_ref, wide, coef, terms, halos
):
    rows, lon = kappa_ref.shape
    probe_local = probes_ref.shape[0] // rows
    total = rows + 2 * SMOOTH
    halves = lon // BLK
    widen(probes_ref, wide)
    terms[...] = own_ref[...].astype(F32) + core_ref[...].astype(F32) + far_ref[...].astype(F32)
    halos[0] = top_ref[...].astype(F32)
    halos[1] = bottom_ref[...].astype(F32)
    lane = lax.broadcasted_iota(jnp.int32, (SUB, lon), 1)
    for r, k in enumerate(kappa_rows(kappa_ref, above_ref, below_ref, probe_local)):
        coef[r] = jnp.broadcast_to(k, (SUB, lon))
    in_grid = [inside[0]] * SMOOTH + [None] * rows + [inside[1]] * SMOOTH

    def joined(ref, first, base):
        return jnp.concatenate([ref[first + h, pl.ds(base, SUB), :] for h in range(halves)], axis=1)

    @pl.loop(0, probe_local // SUB)
    def _(c):
        base = pl.multiple_of(c * SUB, SUB)
        f = (
            [joined(halos.at[0], r * halves, base) for r in range(SMOOTH)]
            + [joined(terms, r * halves, base) for r in range(rows)]
            + [joined(halos.at[1], r * halves, base) for r in range(SMOOTH)]
        )
        for step in range(SMOOTH):
            g = [coef[r] * f[r] for r in range(total)]
            new = list(f)
            for r in range(step + 1, total - step - 1):
                west = jnp.where(lane > 0, pltpu.roll(g[r], 1, 1), 0.0)
                east = jnp.where(lane < lon - 1, pltpu.roll(g[r], lon - 1, 1), 0.0)
                lap = g[r - 1] + g[r + 1] + west + east - 4.0 * g[r]
                if in_grid[r] is not None:
                    lap = lap * in_grid[r]
                new[r] = f[r] + lap
            f = new
        for r in range(rows):
            at = pl.ds(base * rows + r, SUB, stride=rows)
            for h in range(halves):
                wide[h, at, :] += f[r + SMOOTH][:, h * BLK : (h + 1) * BLK]

    for h in range(halves):
        out_ref[:, h * BLK : (h + 1) * BLK] = wide[h]


def swap(x, axis, distance):
    size = lax.axis_size(axis)
    return lax.ppermute(x, axis, [(i, i ^ distance) for i in range(size)])


def exchange_edges(north, south):
    size = lax.axis_size("src")
    down = [(i, i + 1) for i in range(size - 1)]
    up = [(j, i) for i, j in down]
    return lax.ppermute(south, "src", down), lax.ppermute(north, "src", up)


def per_device(probes, kappa, footprint, block_source, block_receptor, block_count, obs_weight):
    probe_local, rows, lon = probes.shape
    halves = lon // BLK
    cells = rows * halves
    tiles = lax.axis_size("src")
    me = lax.axis_index("src")
    blocks = footprint.reshape(footprint.shape[2:])
    slots = blocks.shape[0]
    scalars = (block_source.reshape(-1), block_receptor.reshape(-1), block_count.reshape(-1))
    flat = probes.reshape(probe_local * rows, lon)
    pair = 2 * probe_local

    edge = jax.ShapeDtypeStruct((SMOOTH, probe_local + PIECES, lon), BF16)
    north, south = pl.pallas_call(
        edge_kernel,
        out_shape=(edge, edge),
        in_specs=[VMEM, VMEM],
        out_specs=(VMEM, VMEM),
        scratch_shapes=[pltpu.VMEM((halves, probe_local * rows, BLK), F32)],
        compiler_params=params(),
        name="edges",
    )(flat, kappa)
    above, below = exchange_edges(north, south)

    part = jax.ShapeDtypeStruct((cells, probe_local, BLK), BF16)
    own = pl.pallas_call(
        smooth_kernel,
        out_shape=part,
        in_specs=[VMEM] * 4,
        out_specs=VMEM,
        scratch_shapes=[
            pltpu.VMEM((halves, probe_local * rows, BLK), F32),
            pltpu.VMEM((3, rows + 2 * SMOOTH, SUB, lon), F32),
            pltpu.VMEM((2, SMOOTH, probe_local, lon), F32),
            pltpu.VMEM((cells, probe_local, BLK), F32),
        ],
        compiler_params=params(),
        name="smooth",
    )(flat, kappa, above, below)

    def streamed(kernel, operands, outs, total):
        whole = lambda shape: pl.BlockSpec(shape, lambda g, *_: (0,) * len(shape))
        return pl.pallas_call(
            kernel,
            out_shape=outs,
            grid_spec=pltpu.PrefetchScalarGridSpec(
                num_scalar_prefetch=3,
                grid=(slots // GROUP,),
                in_specs=[pl.BlockSpec((GROUP, BLK, BLK), lambda g, *_: (g, 0, 0))]
                + [whole(x.shape) for x in operands],
                out_specs=jax.tree.map(lambda o: whole(o.shape), outs),
                scratch_shapes=[pltpu.VMEM(total, F32)],
            ),
            compiler_params=params(),
            name=kernel.__name__,
        )(*scalars, blocks, *operands)

    def forward(near, far):
        return streamed(
            forward_kernel,
            (near, far),
            jax.ShapeDtypeStruct((RB_LOC, pair, BLK), BF16),
            (RB_LOC + 1, pair, BLK),
        )

    def adjoint(weighted):
        return streamed(adjoint_kernel, (weighted,), (part, part), (cells + 1, pair, BLK))

    share = RB_LOC * pair // tiles
    weights = jnp.broadcast_to(obs_weight.reshape(RB_LOC, 1, BLK), (RB_LOC, pair, BLK))
    weights = lax.dynamic_index_in_dim(weights.reshape(tiles, share, BLK), me, 0, False)

    def summed(evolved):
        terms = lax.all_to_all(evolved.reshape(tiles, share, BLK), "src", 0, 0)
        return (weights * jnp.sum(terms.astype(F32), axis=0)).astype(BF16)

    def spread(weighted):
        sent = jnp.broadcast_to(weighted[None], (tiles, share, BLK))
        return lax.all_to_all(sent, "src", 0, 0).reshape(RB_LOC, pair, BLK)

    other = swap(own, "rcv", 2)
    beside = swap(own, "rcv", 1)
    first = summed(forward(own, beside))
    second = summed(forward(other, swap(other, "rcv", 1)))

    to_other, to_diagonal = adjoint(spread(second))
    both = (to_other.astype(F32) + swap(to_diagonal, "rcv", 1).astype(F32)).astype(BF16)
    from_other = swap(both, "rcv", 2)
    mine, to_beside = adjoint(spread(first))
    from_beside = swap(to_beside, "rcv", 1)

    edge_cells = SMOOTH * halves

    def edge_sum(lo):
        pieces = [lax.slice_in_dim(x, lo, lo + edge_cells, axis=0).astype(F32) for x in (mine, from_beside, from_other)]
        return (pieces[0] + pieces[1] + pieces[2]).astype(BF16)

    top, bottom = exchange_edges(edge_sum(0), edge_sum(cells - edge_cells))
    inside = jnp.stack([me > 0, me < tiles - 1]).astype(F32)
    out = pl.pallas_call(
        back_kernel,
        out_shape=jax.ShapeDtypeStruct((probe_local * rows, lon), F32),
        in_specs=[SMEM] + [VMEM] * 9,
        out_specs=VMEM,
        scratch_shapes=[
            pltpu.VMEM((halves, probe_local * rows, BLK), F32),
            pltpu.VMEM((rows + 2 * SMOOTH, SUB, lon), F32),
            pltpu.VMEM((cells, probe_local, BLK), F32),
            pltpu.VMEM((2, edge_cells, probe_local, BLK), F32),
        ],
        compiler_params=params(),
        name="back",
    )(inside, flat, kappa, above, below, mine, from_beside, from_other, top, bottom)
    return out.reshape(probe_local, rows, lon)


def solution(mesh):
    placed = (
        P("rcv", "src", None),
        P("src", None),
        P("src", "rcv", None, None, None),
        P("src", "rcv", None),
        P("src", "rcv", None),
        P("src", "rcv"),
        P("rcv"),
    )
    return jax.shard_map(
        per_device, mesh=mesh, in_specs=placed, out_specs=P("rcv", "src", None), check_vma=False
    )
```

```python
import jax
import jax.numpy as jnp
from jax import lax
from jax.experimental import pallas as pl
from jax.experimental.pallas import tpu as pltpu
from jax.sharding import PartitionSpec as P

BLK = 128
RB_LOC = 16
SMOOTH = 4
SUB = 8
PIECES = 16
GROUP = 32
F32, BF16 = jnp.float32, jnp.bfloat16
VMEM = pl.BlockSpec(memory_space=pltpu.VMEM)
SMEM = pl.BlockSpec(memory_space=pltpu.SMEM)


def params(mib=24):
    return pltpu.CompilerParams(vmem_limit_bytes=mib * 1024 * 1024)


def widen(probes_ref, wide):
    for h in range(wide.shape[0]):
        wide[h] = probes_ref[:, h * BLK : (h + 1) * BLK].astype(F32)


def one_row(wide, start, size, rows):
    at = pl.ds(start, size, stride=rows)
    return jnp.concatenate([wide[h, at, :] for h in range(wide.shape[0])], axis=1)


def edge_kernel(probes_ref, kappa_ref, north_ref, south_ref, wide):
    rows, lon = kappa_ref.shape
    probe_local = probes_ref.shape[0] // rows
    widen(probes_ref, wide)
    place = lax.broadcasted_iota(jnp.int32, (PIECES, lon), 0)
    for out_ref, first in ((north_ref, 0), (south_ref, rows - SMOOTH)):
        for r in range(SMOOTH):
            out_ref[r, :probe_local, :] = one_row(wide, first + r, probe_local, rows).astype(BF16)
            whole = kappa_ref[first + r : first + r + 1, :]
            high = whole.astype(BF16).astype(F32)
            rest = whole - high
            middle = rest.astype(BF16).astype(F32)
            low = rest - middle
            pieces = jnp.where(place == 0, high, jnp.where(place == 1, middle, jnp.where(place == 2, low, 0.0)))
            out_ref[r, probe_local:, :] = pieces.astype(BF16)


def kappa_rows(kappa_ref, above_ref, below_ref, probe_local):
    def halo(ref, r):
        piece = ref[r, probe_local:, :].astype(F32)
        return piece[0:1] + piece[1:2] + piece[2:3]

    rows = kappa_ref.shape[0]
    return (
        [halo(above_ref, r) for r in range(SMOOTH)]
        + [kappa_ref[r : r + 1, :] for r in range(rows)]
        + [halo(below_ref, r) for r in range(SMOOTH)]
    )


def smooth_kernel(probes_ref, kappa_ref, above_ref, below_ref, field_ref, wide, coef, halos, result):
    rows, lon = kappa_ref.shape
    probe_local = probes_ref.shape[0] // rows
    total = rows + 2 * SMOOTH
    widen(probes_ref, wide)
    halos[0] = above_ref[:, :probe_local, :].astype(F32)
    halos[1] = below_ref[:, :probe_local, :].astype(F32)
    lane = lax.broadcasted_iota(jnp.int32, (SUB, lon), 1)
    for r, k in enumerate(kappa_rows(kappa_ref, above_ref, below_ref, probe_local)):
        k = jnp.broadcast_to(k, (SUB, lon))
        coef[0, r] = k
        coef[1, r] = jnp.where(lane > 0, k, 0.0)
        coef[2, r] = jnp.where(lane < lon - 1, k, 0.0)

    @pl.loop(0, probe_local // SUB)
    def _(c):
        base = pl.multiple_of(c * SUB, SUB)
        f = (
            [halos[0, r, pl.ds(base, SUB), :] for r in range(SMOOTH)]
            + [one_row(wide, base * rows + r, SUB, rows) for r in range(rows)]
            + [halos[1, r, pl.ds(base, SUB), :] for r in range(SMOOTH)]
        )
        for step in range(SMOOTH):
            new = list(f)
            for r in range(step + 1, total - step - 1):
                k, kl, kr = coef[0, r], coef[1, r], coef[2, r]
                g = f[r]
                new[r] = (
                    g
                    + k * (f[r - 1] + f[r + 1] - 4.0 * g)
                    + kl * pltpu.roll(g, 1, 1)
                    + kr * pltpu.roll(g, lon - 1, 1)
                )
            f = new
        for r in range(rows):
            for h in range(lon // BLK):
                result[r * (lon // BLK) + h, pl.ds(base, SUB), :] = f[r + SMOOTH][:, h * BLK : (h + 1) * BLK]

    field_ref[...] = result[...].astype(BF16)


def hold_kernel(blocks_ref, after_ref, held_ref, arrived):
    copy = pltpu.make_async_copy(blocks_ref, held_ref, arrived)
    copy.start()
    copy.wait()


def each_slot(slots, body):
    @pl.loop(0, slots // GROUP)
    def _(g):
        for i in range(GROUP):
            body(g * GROUP + i)


def forward_kernel(
    sources, receptors, count, place, held, near_ref, far_ref, keep_ref, give_ref, turned, total
):
    total[...] = jnp.zeros_like(total)
    for j in range(turned.shape[0]):
        turned[j] = jnp.concatenate([near_ref[j], far_ref[j]], axis=0).T

    spare = total.shape[0] - 1

    def slot(n):
        b = jnp.where(n < count[0], receptors[n], spare)
        total[b] += jnp.dot(held[n], turned[sources[n]], preferred_element_type=F32)

    each_slot(held.shape[0], slot)
    half = keep_ref.shape[0]
    for out_ref, side in ((keep_ref, place[0]), (give_ref, 1 - place[0])):
        for b in range(half):
            out_ref[b] = total[side * half + b].T.astype(BF16)


def adjoint_kernel(
    sources, receptors, count, place, held, mine_ref, theirs_ref, near_ref, far_ref, weighted, total
):
    total[...] = jnp.zeros_like(total)
    pieces, share = mine_ref.shape[:2]
    for side_ref, side in ((mine_ref, place[0]), (theirs_ref, 1 - place[0])):
        for k in range(pieces):
            row = (side * pieces + lax.bitwise_xor(place[1], k)) * share
            weighted[pl.ds(pl.multiple_of(row, share), share), :] = side_ref[k]

    spare = total.shape[0] - 1
    pair = total.shape[1]

    def slot(n):
        j = jnp.where(n < count[0], sources[n], spare)
        entries = weighted[pl.ds(pl.multiple_of(receptors[n] * pair, pair), pair), :]
        total[j] += jnp.dot(entries, held[n], preferred_element_type=F32)

    each_slot(held.shape[0], slot)
    half = near_ref.shape[1]
    near_ref[...] = total[:spare, :half].astype(BF16)
    far_ref[...] = total[:spare, half:].astype(BF16)


def back_kernel(
    inside, probes_ref, kappa_ref, above_ref, below_ref, own_ref, core_ref, far_ref, top_ref, bottom_ref, out_ref, wide, coef, terms, halos
):
    rows, lon = kappa_ref.shape
    probe_local = probes_ref.shape[0] // rows
    total = rows + 2 * SMOOTH
    halves = lon // BLK
    widen(probes_ref, wide)
    terms[...] = own_ref[...].astype(F32) + core_ref[...].astype(F32) + far_ref[...].astype(F32)
    halos[0] = top_ref[...].astype(F32)
    halos[1] = bottom_ref[...].astype(F32)
    lane = lax.broadcasted_iota(jnp.int32, (SUB, lon), 1)
    for r, k in enumerate(kappa_rows(kappa_ref, above_ref, below_ref, probe_local)):
        coef[r] = jnp.broadcast_to(k, (SUB, lon))
    in_grid = [inside[0]] * SMOOTH + [None] * rows + [inside[1]] * SMOOTH

    def joined(ref, first, base):
        return jnp.concatenate([ref[first + h, pl.ds(base, SUB), :] for h in range(halves)], axis=1)

    @pl.loop(0, probe_local // SUB)
    def _(c):
        base = pl.multiple_of(c * SUB, SUB)
        f = (
            [joined(halos.at[0], r * halves, base) for r in range(SMOOTH)]
            + [joined(terms, r * halves, base) for r in range(rows)]
            + [joined(halos.at[1], r * halves, base) for r in range(SMOOTH)]
        )
        for step in range(SMOOTH):
            g = [coef[r] * f[r] for r in range(total)]
            new = list(f)
            for r in range(step + 1, total - step - 1):
                west = jnp.where(lane > 0, pltpu.roll(g[r], 1, 1), 0.0)
                east = jnp.where(lane < lon - 1, pltpu.roll(g[r], lon - 1, 1), 0.0)
                lap = g[r - 1] + g[r + 1] + west + east - 4.0 * g[r]
                if in_grid[r] is not None:
                    lap = lap * in_grid[r]
                new[r] = f[r] + lap
            f = new
        for r in range(rows):
            at = pl.ds(base * rows + r, SUB, stride=rows)
            for h in range(halves):
                wide[h, at, :] += f[r + SMOOTH][:, h * BLK : (h + 1) * BLK]

    for h in range(halves):
        out_ref[:, h * BLK : (h + 1) * BLK] = wide[h]


def swap(x, axis, distance):
    size = lax.axis_size(axis)
    return lax.ppermute(x, axis, [(i, i ^ distance) for i in range(size)])


def far_first(size):
    return sorted(range(1, size), key=lambda k: -k.bit_length())


def exchange_edges(north, south):
    size = lax.axis_size("src")
    down = [(i, i + 1) for i in range(size - 1)]
    up = [(j, i) for i, j in down]
    return lax.ppermute(south, "src", down), lax.ppermute(north, "src", up)


def per_device(probes, kappa, footprint, block_source, block_receptor, block_count, obs_weight):
    probe_local, rows, lon = probes.shape
    halves = lon // BLK
    cells = rows * halves
    tiles = lax.axis_size("src")
    me = lax.axis_index("src")
    blocks = footprint.reshape(footprint.shape[2:])
    slots = blocks.shape[0]
    flat = probes.reshape(probe_local * rows, lon)
    pair = 2 * probe_local

    edge = jax.ShapeDtypeStruct((SMOOTH, probe_local + PIECES, lon), BF16)
    north, south = pl.pallas_call(
        edge_kernel,
        out_shape=(edge, edge),
        in_specs=[VMEM, VMEM],
        out_specs=(VMEM, VMEM),
        scratch_shapes=[pltpu.VMEM((halves, probe_local * rows, BLK), F32)],
        compiler_params=params(),
        name="edges",
    )(flat, kappa)
    above, below = exchange_edges(north, south)

    def hold(after):
        return pl.pallas_call(
            hold_kernel,
            out_shape=jax.ShapeDtypeStruct(blocks.shape, BF16),
            in_specs=[pl.BlockSpec(memory_space=pltpu.HBM), pl.BlockSpec(memory_space=pl.ANY)],
            out_specs=VMEM,
            scratch_shapes=[pltpu.SemaphoreType.DMA],
            compiler_params=params(),
            cost_estimate=pl.CostEstimate(flops=0, bytes_accessed=4 * slots * BLK * BLK, transcendentals=0),
            name="hold",
        )(blocks, after)

    part = jax.ShapeDtypeStruct((cells, probe_local, BLK), BF16)
    own = pl.pallas_call(
        smooth_kernel,
        out_shape=part,
        in_specs=[VMEM] * 4,
        out_specs=VMEM,
        scratch_shapes=[
            pltpu.VMEM((halves, probe_local * rows, BLK), F32),
            pltpu.VMEM((3, rows + 2 * SMOOTH, SUB, lon), F32),
            pltpu.VMEM((2, SMOOTH, probe_local, lon), F32),
            pltpu.VMEM((cells, probe_local, BLK), F32),
        ],
        compiler_params=params(),
        name="smooth",
    )(flat, kappa, above, below)

    side, row = me % 2, me // 2
    place = jnp.stack([side, row]).astype(jnp.int32)
    scalars = (block_source.reshape(-1), block_receptor.reshape(-1), block_count.reshape(-1), place)
    spread_over = tiles // 2
    share = RB_LOC * pair // tiles

    def over_slots(kernel, held, operands, outs, scratch):
        return pl.pallas_call(
            kernel,
            out_shape=outs,
            in_specs=[SMEM] * len(scalars) + [VMEM] * (1 + len(operands)),
            out_specs=jax.tree.map(lambda _: VMEM, outs),
            scratch_shapes=scratch,
            compiler_params=params(),
            cost_estimate=pl.CostEstimate(
                flops=2 * slots * BLK * BLK * pair, bytes_accessed=2 * slots * BLK * BLK, transcendentals=0
            ),
            name=kernel.__name__,
        )(*scalars, held, *operands)

    def forward(held, near, far):
        half = jax.ShapeDtypeStruct((RB_LOC // 2, pair, BLK), BF16)
        return over_slots(
            forward_kernel,
            held,
            (near, far),
            (half, half),
            [pltpu.VMEM((cells, BLK, pair), BF16), pltpu.VMEM((RB_LOC + 1, BLK, pair), F32)],
        )

    def adjoint(held, mine, theirs):
        return over_slots(
            adjoint_kernel,
            held,
            (mine, theirs),
            (part, part),
            [pltpu.VMEM((RB_LOC * pair, BLK), BF16), pltpu.VMEM((cells + 1, pair, BLK), F32)],
        )

    weights = jnp.broadcast_to(obs_weight.reshape(RB_LOC, 1, BLK), (RB_LOC, pair, BLK))
    weights = lax.dynamic_index_in_dim(weights.reshape(2, spread_over, share, BLK), side, 0, False)
    weights = lax.dynamic_index_in_dim(weights, row, 0, False)

    def summed(keep, give):
        got = swap(give, "src", 1)
        pairs = (keep.astype(F32) + got.astype(F32)).astype(BF16).reshape(spread_over, share, BLK)
        picked = lambda k: lax.dynamic_index_in_dim(pairs, lax.bitwise_xor(row, k), 0, False)
        total = picked(0).astype(F32)
        for k in far_first(spread_over):
            total = total + swap(picked(k), "src", 2 * k).astype(F32)
        return (weights * total).astype(BF16)

    def gathered(weighted):
        pieces = {k: swap(weighted, "src", 2 * k) for k in far_first(spread_over)}
        return jnp.stack([weighted] + [pieces[k] for k in range(1, spread_over)])

    def spread(weighted):
        mine = gathered(weighted)
        return mine, swap(mine, "src", 1)

    other = swap(own, "rcv", 2)
    beside = swap(own, "rcv", 1)
    held = hold(own)
    near_keep, near_give = forward(held, own, beside)
    other, near_give = lax.optimization_barrier((other, near_give))
    first = summed(near_keep, near_give)
    second = summed(*forward(held, other, swap(other, "rcv", 1)))

    held = hold(second)
    second_halves = spread(second)
    first, _ = lax.optimization_barrier((first, second_halves[0]))
    first_mine = gathered(first)
    to_other, to_diagonal = adjoint(held, *second_halves)
    both = (to_other.astype(F32) + swap(to_diagonal, "rcv", 1).astype(F32)).astype(BF16)
    first_mine, both = lax.optimization_barrier((first_mine, both))
    from_other = swap(both, "rcv", 2)
    mine, to_beside = adjoint(held, first_mine, swap(first_mine, "src", 1))
    from_beside = swap(to_beside, "rcv", 1)

    edge_cells = SMOOTH * halves

    def edge_sum(lo):
        pieces = [lax.slice_in_dim(x, lo, lo + edge_cells, axis=0).astype(F32) for x in (mine, from_beside, from_other)]
        return (pieces[0] + pieces[1] + pieces[2]).astype(BF16)

    top, bottom = exchange_edges(edge_sum(0), edge_sum(cells - edge_cells))
    inside = jnp.stack([me > 0, me < tiles - 1]).astype(F32)
    out = pl.pallas_call(
        back_kernel,
        out_shape=jax.ShapeDtypeStruct((probe_local * rows, lon), F32),
        in_specs=[SMEM] + [VMEM] * 9,
        out_specs=VMEM,
        scratch_shapes=[
            pltpu.VMEM((halves, probe_local * rows, BLK), F32),
            pltpu.VMEM((rows + 2 * SMOOTH, SUB, lon), F32),
            pltpu.VMEM((cells, probe_local, BLK), F32),
            pltpu.VMEM((2, edge_cells, probe_local, BLK), F32),
        ],
        compiler_params=params(),
        name="back",
    )(inside, flat, kappa, above, below, mine, from_beside, from_other, top, bottom)
    return out.reshape(probe_local, rows, lon)


def solution(mesh):
    placed = (
        P("rcv", "src", None),
        P("src", None),
        P("src", "rcv", None, None, None),
        P("src", "rcv", None),
        P("src", "rcv", None),
        P("src", "rcv"),
        P("rcv"),
    )
    return jax.shard_map(
        per_device, mesh=mesh, in_specs=placed, out_specs=P("rcv", "src", None), check_vma=False
    )
```

```python
import jax
import jax.numpy as jnp
from jax import lax
from jax.experimental import pallas as pl
from jax.experimental.pallas import tpu as pltpu
from jax.sharding import PartitionSpec as P

BLK = 128
RB_LOC = 16
SMOOTH = 4
SUB = 8
PIECES = 16
GROUP = 32
F32, BF16 = jnp.float32, jnp.bfloat16
VMEM = pl.BlockSpec(memory_space=pltpu.VMEM)
SMEM = pl.BlockSpec(memory_space=pltpu.SMEM)


def params(mib=24):
    return pltpu.CompilerParams(vmem_limit_bytes=mib * 1024 * 1024)


def widen(probes_ref, wide):
    for h in range(wide.shape[0]):
        wide[h] = probes_ref[:, h * BLK : (h + 1) * BLK].astype(F32)


def one_row(wide, start, size, rows):
    at = pl.ds(start, size, stride=rows)
    return jnp.concatenate([wide[h, at, :] for h in range(wide.shape[0])], axis=1)


def edge_kernel(probes_ref, kappa_ref, north_ref, south_ref, wide):
    rows, lon = kappa_ref.shape
    probe_local = probes_ref.shape[0] // rows
    widen(probes_ref, wide)
    place = lax.broadcasted_iota(jnp.int32, (PIECES, lon), 0)
    for out_ref, first in ((north_ref, 0), (south_ref, rows - SMOOTH)):
        for r in range(SMOOTH):
            out_ref[r, :probe_local, :] = one_row(wide, first + r, probe_local, rows).astype(BF16)
            whole = kappa_ref[first + r : first + r + 1, :]
            high = whole.astype(BF16).astype(F32)
            rest = whole - high
            middle = rest.astype(BF16).astype(F32)
            low = rest - middle
            pieces = jnp.where(place == 0, high, jnp.where(place == 1, middle, jnp.where(place == 2, low, 0.0)))
            out_ref[r, probe_local:, :] = pieces.astype(BF16)


def kappa_rows(kappa_ref, above_ref, below_ref, probe_local):
    def halo(ref, r):
        piece = ref[r, probe_local:, :].astype(F32)
        return piece[0:1] + piece[1:2] + piece[2:3]

    rows = kappa_ref.shape[0]
    return (
        [halo(above_ref, r) for r in range(SMOOTH)]
        + [kappa_ref[r : r + 1, :] for r in range(rows)]
        + [halo(below_ref, r) for r in range(SMOOTH)]
    )


def put_row(ref, blk, at, row):
    for h in range(row.shape[1] // BLK):
        ref[blk + h, at, :] = row[:, h * BLK : (h + 1) * BLK]


def smooth_step(f, coef, lon, r):
    k, kl, kr = coef[0, r], coef[1, r], coef[2, r]
    g = f[r]
    return g + k * (f[r - 1] + f[r + 1] - 4.0 * g) + kl * pltpu.roll(g, 1, 1) + kr * pltpu.roll(g, lon - 1, 1)


def smooth_coefficients(coef, kappas, lon):
    lane = lax.broadcasted_iota(jnp.int32, (SUB, lon), 1)
    for r, k in enumerate(kappas):
        k = jnp.broadcast_to(k, (SUB, lon))
        coef[0, r] = k
        coef[1, r] = jnp.where(lane > 0, k, 0.0)
        coef[2, r] = jnp.where(lane < lon - 1, k, 0.0)


def keep_state(state_ref, step, f, at):
    rows = len(f)
    for i in range(2):
        state_ref[0, step, i, at, :] = f[step + i]
        state_ref[1, step, i, at, :] = f[rows - 2 - step + i]


def smooth_inner_kernel(probes_ref, kappa_ref, field_ref, state_ref, wide, coef, result):
    rows, lon = kappa_ref.shape
    probe_local = probes_ref.shape[0] // rows
    halves = lon // BLK
    widen(probes_ref, wide)
    smooth_coefficients(coef, [kappa_ref[r : r + 1, :] for r in range(rows)], lon)

    @pl.loop(0, probe_local // SUB)
    def _(c):
        base = pl.multiple_of(c * SUB, SUB)
        at = pl.ds(base, SUB)
        f = [one_row(wide, base * rows + r, SUB, rows) for r in range(rows)]
        for step in range(SMOOTH):
            keep_state(state_ref, step, f, at)
            f = [smooth_step(f, coef, lon, r) if step < r < rows - 1 - step else f[r] for r in range(rows)]
        for r in range(SMOOTH, rows - SMOOTH):
            put_row(result, (r - SMOOTH) * halves, at, f[r])

    field_ref[...] = result[...].astype(BF16)


def side_rows(state_ref, side, step, mine, at):
    inner = [state_ref[side, step, i, at, :] for i in range(2)]
    return mine + inner if side == 0 else inner + mine


def smooth_outer_kernel(kappa_ref, above_ref, below_ref, state_ref, field_ref, coef, halos, result):
    rows, lon = kappa_ref.shape
    probe_local = state_ref.shape[3]
    halves = lon // BLK
    halos[0] = above_ref[:, :probe_local, :].astype(F32)
    halos[1] = below_ref[:, :probe_local, :].astype(F32)
    smooth_coefficients(coef, kappa_rows(kappa_ref, above_ref, below_ref, probe_local), lon)
    total = rows + 2 * SMOOTH

    @pl.loop(0, probe_local // SUB)
    def _(c):
        base = pl.multiple_of(c * SUB, SUB)
        at = pl.ds(base, SUB)
        for side in range(2):
            mine = [halos[side, r, at, :] for r in range(SMOOTH)]
            for step in range(SMOOTH):
                f = side_rows(state_ref, side, step, mine, at)
                first = step if side == 0 else total - 6 - step
                rows_at = dict(enumerate(f, first))
                new = range(first + 1, first + 5)
                mine = [smooth_step(rows_at, coef, lon, r) for r in new]
            for r in range(SMOOTH):
                put_row(result, (side * SMOOTH + r) * halves, at, mine[r])

    field_ref[...] = result[...].astype(BF16)


def hold_kernel(blocks_ref, after_ref, held_ref, arrived):
    copy = pltpu.make_async_copy(blocks_ref, held_ref, arrived)
    copy.start()
    copy.wait()


def each_slot(slots, body):
    @pl.loop(0, slots // GROUP)
    def _(g):
        for i in range(GROUP):
            body(g * GROUP + i)


def forward_kernel(
    sources, receptors, count, place, held, near_in, near_out, far_in, far_out, keep_ref, give_ref, turned, total
):
    total[...] = jnp.zeros_like(total)
    edge = near_out.shape[0] // 2
    for j in range(turned.shape[0]):
        if edge <= j < turned.shape[0] - edge:
            near, far = near_in[j - edge], far_in[j - edge]
        else:
            at = j if j < edge else j - near_in.shape[0]
            near, far = near_out[at], far_out[at]
        turned[j] = jnp.concatenate([near, far], axis=0).T

    spare = total.shape[0] - 1

    def slot(n):
        b = jnp.where(n < count[0], receptors[n], spare)
        total[b] += jnp.dot(held[n], turned[sources[n]], preferred_element_type=F32)

    each_slot(held.shape[0], slot)
    half = keep_ref.shape[0]
    for out_ref, side in ((keep_ref, place[0]), (give_ref, 1 - place[0])):
        for b in range(half):
            out_ref[b] = total[side * half + b].T.astype(BF16)


def adjoint_kernel(
    sources, receptors, count, place, held, mine_ref, theirs_ref, near_in, near_out, far_in, far_out, weighted, total
):
    total[...] = jnp.zeros_like(total)
    pieces, share = mine_ref.shape[:2]
    for side_ref, side in ((mine_ref, place[0]), (theirs_ref, 1 - place[0])):
        for k in range(pieces):
            row = (side * pieces + lax.bitwise_xor(place[1], k)) * share
            weighted[pl.ds(pl.multiple_of(row, share), share), :] = side_ref[k]

    spare = total.shape[0] - 1
    pair = total.shape[1]

    def slot(n):
        j = jnp.where(n < count[0], sources[n], spare)
        entries = weighted[pl.ds(pl.multiple_of(receptors[n] * pair, pair), pair), :]
        total[j] += jnp.dot(entries, held[n], preferred_element_type=F32)

    each_slot(held.shape[0], slot)
    half = near_in.shape[1]
    edge = near_out.shape[0] // 2
    for at, in_ref, out_ref in ((pl.ds(0, half), near_in, near_out), (pl.ds(half, half), far_in, far_out)):
        out_ref[:edge] = total[:edge, at].astype(BF16)
        in_ref[...] = total[edge : spare - edge, at].astype(BF16)
        out_ref[edge:] = total[spare - edge : spare, at].astype(BF16)


def joined(ref, first, at, halves):
    return jnp.concatenate([ref[first + h, at, :] for h in range(halves)], axis=1)


def back_step(f, g, lane, r):
    lon = lane.shape[1]
    west = jnp.where(lane > 0, pltpu.roll(g[r], 1, 1), 0.0)
    east = jnp.where(lane < lon - 1, pltpu.roll(g[r], lon - 1, 1), 0.0)
    return g[r - 1] + g[r + 1] + west + east - 4.0 * g[r]


def back_inner_kernel(
    probes_ref, kappa_ref, own_in, core_in, far_in, own_out, core_out, far_out, wide, state_ref, coef, terms
):
    rows, lon = kappa_ref.shape
    probe_local = probes_ref.shape[0] // rows
    halves = lon // BLK
    edge = own_out.shape[0] // 2
    widen(probes_ref, wide)
    inner = own_in[...].astype(F32) + core_in[...].astype(F32) + far_in[...].astype(F32)
    outer = own_out[...].astype(F32) + core_out[...].astype(F32) + far_out[...].astype(F32)
    terms[:edge] = outer[:edge]
    terms[edge : terms.shape[0] - edge] = inner
    terms[terms.shape[0] - edge :] = outer[edge:]
    lane = lax.broadcasted_iota(jnp.int32, (SUB, lon), 1)
    for r in range(rows):
        coef[r] = jnp.broadcast_to(kappa_ref[r : r + 1, :], (SUB, lon))

    @pl.loop(0, probe_local // SUB)
    def _(c):
        base = pl.multiple_of(c * SUB, SUB)
        at = pl.ds(base, SUB)
        f = [joined(terms, r * halves, at, halves) for r in range(rows)]
        for step in range(SMOOTH):
            keep_state(state_ref, step, f, at)
            g = {r: coef[r] * f[r] for r in range(step, rows - step)}
            f = [f[r] + back_step(f, g, lane, r) if step < r < rows - 1 - step else f[r] for r in range(rows)]
        for r in range(SMOOTH, rows - SMOOTH):
            for h in range(halves):
                wide[h, pl.ds(base * rows + r, SUB, stride=rows), :] += f[r][:, h * BLK : (h + 1) * BLK]


def back_outer_kernel(
    inside, kappa_ref, above_ref, below_ref, top_ref, bottom_ref, state_ref, done_ref, out_ref, wide, coef, halos
):
    rows, lon = kappa_ref.shape
    probe_local = state_ref.shape[3]
    halves = lon // BLK
    total = rows + 2 * SMOOTH
    wide[...] = done_ref[...]
    halos[0] = top_ref[...].astype(F32)
    halos[1] = bottom_ref[...].astype(F32)
    lane = lax.broadcasted_iota(jnp.int32, (SUB, lon), 1)
    for r, k in enumerate(kappa_rows(kappa_ref, above_ref, below_ref, probe_local)):
        coef[r] = jnp.broadcast_to(k, (SUB, lon))

    @pl.loop(0, probe_local // SUB)
    def _(c):
        base = pl.multiple_of(c * SUB, SUB)
        at = pl.ds(base, SUB)
        for side in range(2):
            mine = [joined(halos.at[side], r * halves, at, halves) for r in range(SMOOTH)]
            for step in range(SMOOTH):
                first = step if side == 0 else total - 6 - step
                f = dict(enumerate(side_rows(state_ref, side, step, mine, at), first))
                g = {r: coef[r] * f[r] for r in f}
                mine = []
                for r in range(first + 1, first + 5):
                    lap = back_step(f, g, lane, r)
                    mine.append(f[r] + (lap if SMOOTH <= r < total - SMOOTH else lap * inside[side]))
            for r in range(SMOOTH):
                row = r if side == 0 else rows - SMOOTH + r
                for h in range(halves):
                    wide[h, pl.ds(base * rows + row, SUB, stride=rows), :] += mine[r][:, h * BLK : (h + 1) * BLK]

    for h in range(halves):
        out_ref[:, h * BLK : (h + 1) * BLK] = wide[h]


def swap(x, axis, distance):
    size = lax.axis_size(axis)
    return lax.ppermute(x, axis, [(i, i ^ distance) for i in range(size)])


def far_first(size):
    return sorted(range(1, size), key=lambda k: -k.bit_length())


def exchange_edges(north, south):
    size = lax.axis_size("src")
    down = [(i, i + 1) for i in range(size - 1)]
    up = [(j, i) for i, j in down]
    return lax.ppermute(south, "src", down), lax.ppermute(north, "src", up)


def per_device(probes, kappa, footprint, block_source, block_receptor, block_count, obs_weight):
    probe_local, rows, lon = probes.shape
    halves = lon // BLK
    cells = rows * halves
    tiles = lax.axis_size("src")
    me = lax.axis_index("src")
    blocks = footprint.reshape(footprint.shape[2:])
    slots = blocks.shape[0]
    flat = probes.reshape(probe_local * rows, lon)
    pair = 2 * probe_local

    edge = jax.ShapeDtypeStruct((SMOOTH, probe_local + PIECES, lon), BF16)
    north, south = pl.pallas_call(
        edge_kernel,
        out_shape=(edge, edge),
        in_specs=[VMEM, VMEM],
        out_specs=(VMEM, VMEM),
        scratch_shapes=[pltpu.VMEM((halves, probe_local * rows, BLK), F32)],
        compiler_params=params(),
        name="edges",
    )(flat, kappa)
    above, below = exchange_edges(north, south)

    def hold(after):
        return pl.pallas_call(
            hold_kernel,
            out_shape=jax.ShapeDtypeStruct(blocks.shape, BF16),
            in_specs=[pl.BlockSpec(memory_space=pltpu.HBM), pl.BlockSpec(memory_space=pl.ANY)],
            out_specs=VMEM,
            scratch_shapes=[pltpu.SemaphoreType.DMA],
            compiler_params=params(),
            cost_estimate=pl.CostEstimate(flops=0, bytes_accessed=4 * slots * BLK * BLK, transcendentals=0),
            name="hold",
        )(blocks, after)

    edge_cells = SMOOTH * halves
    inner_part = jax.ShapeDtypeStruct((cells - 2 * edge_cells, probe_local, BLK), BF16)
    outer_part = jax.ShapeDtypeStruct((2 * edge_cells, probe_local, BLK), BF16)
    state = jax.ShapeDtypeStruct((2, SMOOTH, 2, probe_local, lon), F32)
    by_half = (halves, probe_local * rows, BLK)
    halo_rows = rows + 2 * SMOOTH
    own_in, smooth_state = pl.pallas_call(
        smooth_inner_kernel,
        out_shape=(inner_part, state),
        in_specs=[VMEM] * 2,
        out_specs=(VMEM, VMEM),
        scratch_shapes=[
            pltpu.VMEM(by_half, F32),
            pltpu.VMEM((3, rows, SUB, lon), F32),
            pltpu.VMEM(inner_part.shape, F32),
        ],
        compiler_params=params(),
        name="smooth_inner",
    )(flat, kappa)
    own_out = pl.pallas_call(
        smooth_outer_kernel,
        out_shape=outer_part,
        in_specs=[VMEM] * 4,
        out_specs=VMEM,
        scratch_shapes=[
            pltpu.VMEM((3, halo_rows, SUB, lon), F32),
            pltpu.VMEM((2, SMOOTH, probe_local, lon), F32),
            pltpu.VMEM(outer_part.shape, F32),
        ],
        compiler_params=params(),
        name="smooth_outer",
    )(kappa, above, below, smooth_state)

    side, row = me % 2, me // 2
    place = jnp.stack([side, row]).astype(jnp.int32)
    scalars = (block_source.reshape(-1), block_receptor.reshape(-1), block_count.reshape(-1), place)
    spread_over = tiles // 2
    share = RB_LOC * pair // tiles

    def over_slots(kernel, held, operands, outs, scratch):
        return pl.pallas_call(
            kernel,
            out_shape=outs,
            in_specs=[SMEM] * len(scalars) + [VMEM] * (1 + len(operands)),
            out_specs=jax.tree.map(lambda _: VMEM, outs),
            scratch_shapes=scratch,
            compiler_params=params(),
            cost_estimate=pl.CostEstimate(
                flops=2 * slots * BLK * BLK * pair, bytes_accessed=2 * slots * BLK * BLK, transcendentals=0
            ),
            name=kernel.__name__,
        )(*scalars, held, *operands)

    def forward(held, *fields):
        half = jax.ShapeDtypeStruct((RB_LOC // 2, pair, BLK), BF16)
        return over_slots(
            forward_kernel,
            held,
            fields,
            (half, half),
            [pltpu.VMEM((cells, BLK, pair), BF16), pltpu.VMEM((RB_LOC + 1, BLK, pair), F32)],
        )

    def adjoint(held, mine, theirs):
        return over_slots(
            adjoint_kernel,
            held,
            (mine, theirs),
            (inner_part, outer_part) * 2,
            [pltpu.VMEM((RB_LOC * pair, BLK), BF16), pltpu.VMEM((cells + 1, pair, BLK), F32)],
        )

    weights = jnp.broadcast_to(obs_weight.reshape(RB_LOC, 1, BLK), (RB_LOC, pair, BLK))
    weights = lax.dynamic_index_in_dim(weights.reshape(2, spread_over, share, BLK), side, 0, False)
    weights = lax.dynamic_index_in_dim(weights, row, 0, False)

    def summed(keep, give):
        got = swap(give, "src", 1)
        pairs = (keep.astype(F32) + got.astype(F32)).astype(BF16).reshape(spread_over, share, BLK)
        picked = lambda k: lax.dynamic_index_in_dim(pairs, lax.bitwise_xor(row, k), 0, False)
        total = picked(0).astype(F32)
        for k in far_first(spread_over):
            total = total + swap(picked(k), "src", 2 * k).astype(F32)
        return (weights * total).astype(BF16)

    def gathered(weighted):
        pieces = {k: swap(weighted, "src", 2 * k) for k in far_first(spread_over)}
        return jnp.stack([weighted] + [pieces[k] for k in range(1, spread_over)])

    def spread(weighted):
        mine = gathered(weighted)
        return mine, swap(mine, "src", 1)

    own = (own_in, own_out)
    other = [swap(x, "rcv", 2) for x in own]
    beside = [swap(x, "rcv", 1) for x in own]
    held = hold(own_out)
    near_keep, near_give = forward(held, *own, *beside)
    other[1], near_give = lax.optimization_barrier((other[1], near_give))
    first = summed(near_keep, near_give)
    second = summed(*forward(held, *other, *[swap(x, "rcv", 1) for x in other]))

    held = hold(second)
    second_halves = spread(second)
    first_halves = spread(first)
    mine_in, mine_out, *to_beside = adjoint(held, *first_halves)
    beside_in, beside_out = [swap(x, "rcv", 1) for x in to_beside]
    other_in, other_out, diagonal_in, diagonal_out = adjoint(held, *second_halves)
    both = lambda here, there: (here.astype(F32) + swap(there, "rcv", 1).astype(F32)).astype(BF16)
    far_out = swap(both(other_out, diagonal_out), "rcv", 2)
    far_in = swap(both(other_in, diagonal_in), "rcv", 2)

    edges = (mine_out.astype(F32) + beside_out.astype(F32) + far_out.astype(F32)).astype(BF16)
    top, bottom = exchange_edges(edges[:edge_cells], edges[edge_cells:])
    inside = jnp.stack([me > 0, me < tiles - 1]).astype(F32)
    inner, back_state = pl.pallas_call(
        back_inner_kernel,
        out_shape=(jax.ShapeDtypeStruct(by_half, F32), state),
        in_specs=[VMEM] * 8,
        out_specs=(VMEM, VMEM),
        scratch_shapes=[pltpu.VMEM((rows, SUB, lon), F32), pltpu.VMEM((cells, probe_local, BLK), F32)],
        compiler_params=params(),
        name="back_inner",
    )(flat, kappa, mine_in, beside_in, far_in, mine_out, beside_out, far_out)
    out = pl.pallas_call(
        back_outer_kernel,
        out_shape=jax.ShapeDtypeStruct((probe_local * rows, lon), F32),
        in_specs=[SMEM] + [VMEM] * 7,
        out_specs=VMEM,
        scratch_shapes=[
            pltpu.VMEM(by_half, F32),
            pltpu.VMEM((halo_rows, SUB, lon), F32),
            pltpu.VMEM((2, edge_cells, probe_local, BLK), F32),
        ],
        compiler_params=params(),
        name="back_outer",
    )(inside, kappa, above, below, top, bottom, back_state, inner)
    return out.reshape(probe_local, rows, lon)


def solution(mesh):
    placed = (
        P("rcv", "src", None),
        P("src", None),
        P("src", "rcv", None, None, None),
        P("src", "rcv", None),
        P("src", "rcv", None),
        P("src", "rcv"),
        P("rcv"),
    )
    return jax.shard_map(
        per_device, mesh=mesh, in_specs=placed, out_specs=P("rcv", "src", None), check_vma=False
    )
```

```python
import jax
import jax.numpy as jnp
from jax import lax
from jax.experimental import pallas as pl
from jax.experimental.pallas import tpu as pltpu
from jax.sharding import PartitionSpec as P

BLK = 128
RB_LOC = 16
SMOOTH = 4
SUB = 8
PIECES = 16
GROUP = 32
F32, BF16 = jnp.float32, jnp.bfloat16
VMEM = pl.BlockSpec(memory_space=pltpu.VMEM)
SMEM = pl.BlockSpec(memory_space=pltpu.SMEM)


def params(mib=24):
    return pltpu.CompilerParams(vmem_limit_bytes=mib * 1024 * 1024)


def widen(probes_ref, wide):
    for h in range(wide.shape[0]):
        wide[h] = probes_ref[:, h * BLK : (h + 1) * BLK].astype(F32)


def one_row(wide, start, size, rows):
    at = pl.ds(start, size, stride=rows)
    return jnp.concatenate([wide[h, at, :] for h in range(wide.shape[0])], axis=1)


def edge_kernel(probes_ref, kappa_ref, north_ref, south_ref, wide):
    rows, lon = kappa_ref.shape
    probe_local = probes_ref.shape[0] // rows
    widen(probes_ref, wide)
    place = lax.broadcasted_iota(jnp.int32, (PIECES, lon), 0)
    for out_ref, first in ((north_ref, 0), (south_ref, rows - SMOOTH)):
        for r in range(SMOOTH):
            out_ref[r, :probe_local, :] = one_row(wide, first + r, probe_local, rows).astype(BF16)
            whole = kappa_ref[first + r : first + r + 1, :]
            high = whole.astype(BF16).astype(F32)
            rest = whole - high
            middle = rest.astype(BF16).astype(F32)
            low = rest - middle
            pieces = jnp.where(place == 0, high, jnp.where(place == 1, middle, jnp.where(place == 2, low, 0.0)))
            out_ref[r, probe_local:, :] = pieces.astype(BF16)


def kappa_rows(kappa_ref, above_ref, below_ref, probe_local):
    def halo(ref, r):
        piece = ref[r, probe_local:, :].astype(F32)
        return piece[0:1] + piece[1:2] + piece[2:3]

    rows = kappa_ref.shape[0]
    return (
        [halo(above_ref, r) for r in range(SMOOTH)]
        + [kappa_ref[r : r + 1, :] for r in range(rows)]
        + [halo(below_ref, r) for r in range(SMOOTH)]
    )


def put_row(ref, blk, at, row):
    for h in range(row.shape[1] // BLK):
        ref[blk + h, at, :] = row[:, h * BLK : (h + 1) * BLK]


def smooth_step(f, coef, lon, r):
    k, kl, kr = coef[0, r], coef[1, r], coef[2, r]
    g = f[r]
    return g + k * (f[r - 1] + f[r + 1] - 4.0 * g) + kl * pltpu.roll(g, 1, 1) + kr * pltpu.roll(g, lon - 1, 1)


def smooth_coefficients(coef, kappas, lon):
    lane = lax.broadcasted_iota(jnp.int32, (SUB, lon), 1)
    for r, k in enumerate(kappas):
        k = jnp.broadcast_to(k, (SUB, lon))
        coef[0, r] = k
        coef[1, r] = jnp.where(lane > 0, k, 0.0)
        coef[2, r] = jnp.where(lane < lon - 1, k, 0.0)


def keep_state(state_ref, step, f, at):
    rows = len(f)
    for i in range(2):
        state_ref[0, step, i, at, :] = f[step + i]
        state_ref[1, step, i, at, :] = f[rows - 2 - step + i]


def smooth_inner_kernel(probes_ref, kappa_ref, field_ref, state_ref, wide, coef, result):
    rows, lon = kappa_ref.shape
    probe_local = probes_ref.shape[0] // rows
    halves = lon // BLK
    widen(probes_ref, wide)
    smooth_coefficients(coef, [kappa_ref[r : r + 1, :] for r in range(rows)], lon)

    @pl.loop(0, probe_local // SUB)
    def _(c):
        base = pl.multiple_of(c * SUB, SUB)
        at = pl.ds(base, SUB)
        f = [one_row(wide, base * rows + r, SUB, rows) for r in range(rows)]
        for step in range(SMOOTH):
            keep_state(state_ref, step, f, at)
            f = [smooth_step(f, coef, lon, r) if step < r < rows - 1 - step else f[r] for r in range(rows)]
        for r in range(SMOOTH, rows - SMOOTH):
            put_row(result, (r - SMOOTH) * halves, at, f[r])

    field_ref[...] = result[...].astype(BF16)


def side_rows(state_ref, side, step, mine, at):
    inner = [state_ref[side, step, i, at, :] for i in range(2)]
    return mine + inner if side == 0 else inner + mine


def smooth_outer_kernel(kappa_ref, above_ref, below_ref, state_ref, field_ref, coef, halos, result):
    rows, lon = kappa_ref.shape
    probe_local = state_ref.shape[3]
    halves = lon // BLK
    halos[0] = above_ref[:, :probe_local, :].astype(F32)
    halos[1] = below_ref[:, :probe_local, :].astype(F32)
    smooth_coefficients(coef, kappa_rows(kappa_ref, above_ref, below_ref, probe_local), lon)
    total = rows + 2 * SMOOTH

    @pl.loop(0, probe_local // SUB)
    def _(c):
        base = pl.multiple_of(c * SUB, SUB)
        at = pl.ds(base, SUB)
        for side in range(2):
            mine = [halos[side, r, at, :] for r in range(SMOOTH)]
            for step in range(SMOOTH):
                f = side_rows(state_ref, side, step, mine, at)
                first = step if side == 0 else total - 6 - step
                rows_at = dict(enumerate(f, first))
                new = range(first + 1, first + 5)
                mine = [smooth_step(rows_at, coef, lon, r) for r in new]
            for r in range(SMOOTH):
                put_row(result, (side * SMOOTH + r) * halves, at, mine[r])

    field_ref[...] = result[...].astype(BF16)


def hold_kernel(blocks_ref, after_ref, held_ref, arrived):
    copy = pltpu.make_async_copy(blocks_ref, held_ref, arrived)
    copy.start()
    copy.wait()


def each_slot(slots, body):
    @pl.loop(0, slots // GROUP)
    def _(g):
        for i in range(GROUP):
            body(g * GROUP + i)


def forward_kernel(
    sources, receptors, count, place, held, near_in, near_out, far_in, far_out, keep_ref, give_ref, turned, total
):
    total[...] = jnp.zeros_like(total)
    edge = near_out.shape[0] // 2
    for j in range(turned.shape[0]):
        if edge <= j < turned.shape[0] - edge:
            near, far = near_in[j - edge], far_in[j - edge]
        else:
            at = j if j < edge else j - near_in.shape[0]
            near, far = near_out[at], far_out[at]
        turned[j] = jnp.concatenate([near, far], axis=0).T

    spare = total.shape[0] - 1

    def slot(n):
        b = jnp.where(n < count[0], receptors[n], spare)
        total[b] += jnp.dot(held[n], turned[sources[n]], preferred_element_type=F32)

    each_slot(held.shape[0], slot)
    half = keep_ref.shape[0]
    for out_ref, side in ((keep_ref, place[0]), (give_ref, 1 - place[0])):
        for b in range(half):
            out_ref[b] = total[side * half + b].T.astype(BF16)


def adjoint_kernel(
    sources, receptors, count, place, held, mine_ref, theirs_ref, near_in, near_out, far_in, far_out, weighted, total
):
    total[...] = jnp.zeros_like(total)
    pieces, share = mine_ref.shape[:2]
    for side_ref, side in ((mine_ref, place[0]), (theirs_ref, 1 - place[0])):
        for k in range(pieces):
            row = (side * pieces + lax.bitwise_xor(place[1], k)) * share
            weighted[pl.ds(pl.multiple_of(row, share), share), :] = side_ref[k]

    spare = total.shape[0] - 1
    pair = total.shape[1]

    def slot(n):
        j = jnp.where(n < count[0], sources[n], spare)
        entries = weighted[pl.ds(pl.multiple_of(receptors[n] * pair, pair), pair), :]
        total[j] += jnp.dot(entries, held[n], preferred_element_type=F32)

    each_slot(held.shape[0], slot)
    half = near_in.shape[1]
    edge = near_out.shape[0] // 2
    for at, in_ref, out_ref in ((pl.ds(0, half), near_in, near_out), (pl.ds(half, half), far_in, far_out)):
        out_ref[:edge] = total[:edge, at].astype(BF16)
        in_ref[...] = total[edge : spare - edge, at].astype(BF16)
        out_ref[edge:] = total[spare - edge : spare, at].astype(BF16)


def joined(ref, first, at, halves):
    return jnp.concatenate([ref[first + h, at, :] for h in range(halves)], axis=1)


def back_step(f, g, lane, r):
    lon = lane.shape[1]
    west = jnp.where(lane > 0, pltpu.roll(g[r], 1, 1), 0.0)
    east = jnp.where(lane < lon - 1, pltpu.roll(g[r], lon - 1, 1), 0.0)
    return g[r - 1] + g[r + 1] + west + east - 4.0 * g[r]


def back_inner_kernel(
    probes_ref, kappa_ref, own_in, core_in, far_in, own_out, core_out, far_out, wide, state_ref, coef, terms
):
    rows, lon = kappa_ref.shape
    probe_local = probes_ref.shape[0] // rows
    halves = lon // BLK
    edge = own_out.shape[0] // 2
    widen(probes_ref, wide)
    inner = own_in[...].astype(F32) + core_in[...].astype(F32) + far_in[...].astype(F32)
    outer = own_out[...].astype(F32) + core_out[...].astype(F32) + far_out[...].astype(F32)
    terms[:edge] = outer[:edge]
    terms[edge : terms.shape[0] - edge] = inner
    terms[terms.shape[0] - edge :] = outer[edge:]
    lane = lax.broadcasted_iota(jnp.int32, (SUB, lon), 1)
    for r in range(rows):
        coef[r] = jnp.broadcast_to(kappa_ref[r : r + 1, :], (SUB, lon))

    @pl.loop(0, probe_local // SUB)
    def _(c):
        base = pl.multiple_of(c * SUB, SUB)
        at = pl.ds(base, SUB)
        f = [joined(terms, r * halves, at, halves) for r in range(rows)]
        for step in range(SMOOTH):
            keep_state(state_ref, step, f, at)
            g = {r: coef[r] * f[r] for r in range(step, rows - step)}
            f = [f[r] + back_step(f, g, lane, r) if step < r < rows - 1 - step else f[r] for r in range(rows)]
        for r in range(SMOOTH, rows - SMOOTH):
            for h in range(halves):
                wide[h, pl.ds(base * rows + r, SUB, stride=rows), :] += f[r][:, h * BLK : (h + 1) * BLK]


def back_outer_kernel(
    inside, kappa_ref, above_ref, below_ref, top_ref, bottom_ref, state_ref, done_ref, out_ref, wide, coef, halos
):
    rows, lon = kappa_ref.shape
    probe_local = state_ref.shape[3]
    halves = lon // BLK
    total = rows + 2 * SMOOTH
    wide[...] = done_ref[...]
    halos[0] = top_ref[...].astype(F32)
    halos[1] = bottom_ref[...].astype(F32)
    lane = lax.broadcasted_iota(jnp.int32, (SUB, lon), 1)
    for r, k in enumerate(kappa_rows(kappa_ref, above_ref, below_ref, probe_local)):
        coef[r] = jnp.broadcast_to(k, (SUB, lon))

    @pl.loop(0, probe_local // SUB)
    def _(c):
        base = pl.multiple_of(c * SUB, SUB)
        at = pl.ds(base, SUB)
        for side in range(2):
            mine = [joined(halos.at[side], r * halves, at, halves) for r in range(SMOOTH)]
            for step in range(SMOOTH):
                first = step if side == 0 else total - 6 - step
                f = dict(enumerate(side_rows(state_ref, side, step, mine, at), first))
                g = {r: coef[r] * f[r] for r in f}
                mine = []
                for r in range(first + 1, first + 5):
                    lap = back_step(f, g, lane, r)
                    mine.append(f[r] + (lap if SMOOTH <= r < total - SMOOTH else lap * inside[side]))
            for r in range(SMOOTH):
                row = r if side == 0 else rows - SMOOTH + r
                for h in range(halves):
                    wide[h, pl.ds(base * rows + row, SUB, stride=rows), :] += mine[r][:, h * BLK : (h + 1) * BLK]

    for h in range(halves):
        out_ref[:, h * BLK : (h + 1) * BLK] = wide[h]


def swap(x, axis, distance):
    size = lax.axis_size(axis)
    return lax.ppermute(x, axis, [(i, i ^ distance) for i in range(size)])


def far_first(size):
    return sorted(range(1, size), key=lambda k: -k.bit_length())


def exchange_edges(north, south):
    size = lax.axis_size("src")
    down = [(i, i + 1) for i in range(size - 1)]
    up = [(j, i) for i, j in down]
    return lax.ppermute(south, "src", down), lax.ppermute(north, "src", up)


def per_device(probes, kappa, footprint, block_source, block_receptor, block_count, obs_weight):
    probe_local, rows, lon = probes.shape
    halves = lon // BLK
    cells = rows * halves
    tiles = lax.axis_size("src")
    me = lax.axis_index("src")
    blocks = footprint.reshape(footprint.shape[2:])
    slots = blocks.shape[0]
    flat = probes.reshape(probe_local * rows, lon)
    pair = 2 * probe_local

    edge = jax.ShapeDtypeStruct((SMOOTH, probe_local + PIECES, lon), BF16)
    north, south = pl.pallas_call(
        edge_kernel,
        out_shape=(edge, edge),
        in_specs=[VMEM, VMEM],
        out_specs=(VMEM, VMEM),
        scratch_shapes=[pltpu.VMEM((halves, probe_local * rows, BLK), F32)],
        compiler_params=params(),
        name="edges",
    )(flat, kappa)
    above, below = exchange_edges(north, south)

    def hold(after):
        return pl.pallas_call(
            hold_kernel,
            out_shape=jax.ShapeDtypeStruct(blocks.shape, BF16),
            in_specs=[pl.BlockSpec(memory_space=pltpu.HBM), pl.BlockSpec(memory_space=pl.ANY)],
            out_specs=VMEM,
            scratch_shapes=[pltpu.SemaphoreType.DMA],
            compiler_params=params(),
            cost_estimate=pl.CostEstimate(flops=0, bytes_accessed=4 * slots * BLK * BLK, transcendentals=0),
            name="hold",
        )(pltpu.with_memory_space_constraint(blocks, pltpu.HBM), after)

    edge_cells = SMOOTH * halves
    inner_part = jax.ShapeDtypeStruct((cells - 2 * edge_cells, probe_local, BLK), BF16)
    outer_part = jax.ShapeDtypeStruct((2 * edge_cells, probe_local, BLK), BF16)
    state = jax.ShapeDtypeStruct((2, SMOOTH, 2, probe_local, lon), F32)
    by_half = (halves, probe_local * rows, BLK)
    halo_rows = rows + 2 * SMOOTH
    own_in, smooth_state = pl.pallas_call(
        smooth_inner_kernel,
        out_shape=(inner_part, state),
        in_specs=[VMEM] * 2,
        out_specs=(VMEM, VMEM),
        scratch_shapes=[
            pltpu.VMEM(by_half, F32),
            pltpu.VMEM((3, rows, SUB, lon), F32),
            pltpu.VMEM(inner_part.shape, F32),
        ],
        compiler_params=params(),
        name="smooth_inner",
    )(flat, kappa)
    own_out = pl.pallas_call(
        smooth_outer_kernel,
        out_shape=outer_part,
        in_specs=[VMEM] * 4,
        out_specs=VMEM,
        scratch_shapes=[
            pltpu.VMEM((3, halo_rows, SUB, lon), F32),
            pltpu.VMEM((2, SMOOTH, probe_local, lon), F32),
            pltpu.VMEM(outer_part.shape, F32),
        ],
        compiler_params=params(),
        name="smooth_outer",
    )(kappa, above, below, smooth_state)

    side, row = me % 2, me // 2
    place = jnp.stack([side, row]).astype(jnp.int32)
    scalars = (block_source.reshape(-1), block_receptor.reshape(-1), block_count.reshape(-1), place)
    spread_over = tiles // 2
    share = RB_LOC * pair // tiles

    def over_slots(kernel, held, operands, outs, scratch):
        return pl.pallas_call(
            kernel,
            out_shape=outs,
            in_specs=[SMEM] * len(scalars) + [VMEM] * (1 + len(operands)),
            out_specs=jax.tree.map(lambda _: VMEM, outs),
            scratch_shapes=scratch,
            compiler_params=params(),
            cost_estimate=pl.CostEstimate(
                flops=2 * slots * BLK * BLK * pair, bytes_accessed=2 * slots * BLK * BLK, transcendentals=0
            ),
            name=kernel.__name__,
        )(*scalars, held, *operands)

    def forward(held, *fields):
        half = jax.ShapeDtypeStruct((RB_LOC // 2, pair, BLK), BF16)
        return over_slots(
            forward_kernel,
            held,
            fields,
            (half, half),
            [pltpu.VMEM((cells, BLK, pair), BF16), pltpu.VMEM((RB_LOC + 1, BLK, pair), F32)],
        )

    def adjoint(held, mine, theirs):
        return over_slots(
            adjoint_kernel,
            held,
            (mine, theirs),
            (inner_part, outer_part) * 2,
            [pltpu.VMEM((RB_LOC * pair, BLK), BF16), pltpu.VMEM((cells + 1, pair, BLK), F32)],
        )

    first_row = (side * spread_over + row) * share
    held_blocks = max(share // pair, 1)
    weights = lax.dynamic_slice_in_dim(obs_weight.reshape(RB_LOC, 1, BLK), first_row // pair, held_blocks)
    weights = jnp.broadcast_to(weights, (held_blocks, share // held_blocks, BLK)).reshape(share, BLK)

    def summed(keep, give):
        got = swap(give, "src", 1)
        pairs = (keep.astype(F32) + got.astype(F32)).astype(BF16).reshape(spread_over, share, BLK)
        picked = lambda k: lax.dynamic_index_in_dim(pairs, lax.bitwise_xor(row, k), 0, False)
        total = picked(0).astype(F32)
        for k in far_first(spread_over):
            total = total + swap(picked(k), "src", 2 * k).astype(F32)
        return (weights * total).astype(BF16)

    def gathered(weighted):
        pieces = {k: swap(weighted, "src", 2 * k) for k in far_first(spread_over)}
        return jnp.stack([weighted] + [pieces[k] for k in range(1, spread_over)])

    def spread(weighted):
        mine = gathered(weighted)
        return mine, swap(mine, "src", 1)

    own = (own_in, own_out)
    other = [swap(x, "rcv", 2) for x in own]
    beside = [swap(x, "rcv", 1) for x in own]
    held = hold(own_out)
    near_keep, near_give = forward(held, *own, *beside)
    other[1], near_give = lax.optimization_barrier((other[1], near_give))
    first = summed(near_keep, near_give)
    second = summed(*forward(hold(near_give), *other, *[swap(x, "rcv", 1) for x in other]))

    held = hold(first)
    first_mine = gathered(first)
    second_mine = gathered(second)
    second_mine, _ = lax.optimization_barrier((second_mine, first_mine))
    mine_in, mine_out, *to_beside = adjoint(held, first_mine, swap(first_mine, "src", 1))
    beside_in, beside_out = [swap(x, "rcv", 1) for x in to_beside]
    second_halves = (second_mine, swap(second_mine, "src", 1))
    second_halves, mine_in = lax.optimization_barrier((second_halves, mine_in))
    other_in, other_out, diagonal_in, diagonal_out = adjoint(held, *second_halves)
    both = lambda here, there: (here.astype(F32) + swap(there, "rcv", 1).astype(F32)).astype(BF16)
    far_out = swap(both(other_out, diagonal_out), "rcv", 2)
    far_in = swap(both(other_in, diagonal_in), "rcv", 2)

    edges = (mine_out.astype(F32) + beside_out.astype(F32) + far_out.astype(F32)).astype(BF16)
    top, bottom = exchange_edges(edges[:edge_cells], edges[edge_cells:])
    inside = jnp.stack([me > 0, me < tiles - 1]).astype(F32)
    inner, back_state = pl.pallas_call(
        back_inner_kernel,
        out_shape=(jax.ShapeDtypeStruct(by_half, F32), state),
        in_specs=[VMEM] * 8,
        out_specs=(VMEM, VMEM),
        scratch_shapes=[pltpu.VMEM((rows, SUB, lon), F32), pltpu.VMEM((cells, probe_local, BLK), F32)],
        compiler_params=params(),
        name="back_inner",
    )(flat, kappa, mine_in, beside_in, far_in, mine_out, beside_out, far_out)
    out = pl.pallas_call(
        back_outer_kernel,
        out_shape=jax.ShapeDtypeStruct((probe_local * rows, lon), F32),
        in_specs=[SMEM] + [VMEM] * 7,
        out_specs=VMEM,
        scratch_shapes=[
            pltpu.VMEM(by_half, F32),
            pltpu.VMEM((halo_rows, SUB, lon), F32),
            pltpu.VMEM((2, edge_cells, probe_local, BLK), F32),
        ],
        compiler_params=params(),
        name="back_outer",
    )(inside, kappa, above, below, top, bottom, back_state, inner)
    return out.reshape(probe_local, rows, lon)


def solution(mesh):
    placed = (
        P("rcv", "src", None),
        P("src", None),
        P("src", "rcv", None, None, None),
        P("src", "rcv", None),
        P("src", "rcv", None),
        P("src", "rcv"),
        P("rcv"),
    )
    return jax.shard_map(
        per_device, mesh=mesh, in_specs=placed, out_specs=P("rcv", "src", None), check_vma=False
    )
```

```python
import jax
import jax.numpy as jnp
from jax import lax
from jax.experimental import pallas as pl
from jax.experimental.pallas import tpu as pltpu
from jax.sharding import PartitionSpec as P

BLK = 128
RB_LOC = 16
SMOOTH = 4
SUB = 8
PIECES = 16
GROUP = 32
FETCHES = 4
F32, BF16 = jnp.float32, jnp.bfloat16
VMEM = pl.BlockSpec(memory_space=pltpu.VMEM)
SMEM = pl.BlockSpec(memory_space=pltpu.SMEM)
HBM = pl.BlockSpec(memory_space=pltpu.HBM)


def in_hbm(x):
    return pltpu.with_memory_space_constraint(x, pltpu.HBM)


def params(mib=24):
    return pltpu.CompilerParams(vmem_limit_bytes=mib * 1024 * 1024)


def widen(probes_ref, wide):
    for h in range(wide.shape[0]):
        wide[h] = probes_ref[:, h * BLK : (h + 1) * BLK].astype(F32)


def one_row(wide, start, size, rows):
    at = pl.ds(start, size, stride=rows)
    return [wide[h, at, :] for h in range(wide.shape[0])]


def split_row(row):
    return [row[:, h * BLK : (h + 1) * BLK] for h in range(row.shape[1] // BLK)]


def around(north, row, south, lane):
    east = [pltpu.roll(x, 1, 1) for x in row]
    west = [pltpu.roll(x, BLK - 1, 1) for x in row]
    out = []
    for h, x in enumerate(row):
        left = jnp.where(lane > 0, east[h], east[h - 1] if h else 0.0)
        right = jnp.where(lane < BLK - 1, west[h], west[h + 1] if h + 1 < len(row) else 0.0)
        out.append(((north[h] + south[h]) + (left + right)) - 4.0 * x)
    return out


def edge_kernel(probes_hbm, kappa_hbm, north_ref, south_ref, probes_ref, kappa_ref, wide, arrived):
    fetches = [
        pltpu.make_async_copy(probes_hbm, probes_ref, arrived.at[0]),
        pltpu.make_async_copy(kappa_hbm, kappa_ref, arrived.at[1]),
    ]
    for fetch in fetches:
        fetch.start()
    for fetch in fetches:
        fetch.wait()
    rows, lon = kappa_ref.shape
    probe_local = probes_ref.shape[0] // rows
    widen(probes_ref, wide)
    place = lax.broadcasted_iota(jnp.int32, (PIECES, lon), 0)
    for out_ref, first in ((north_ref, 0), (south_ref, rows - SMOOTH)):
        for r in range(SMOOTH):
            for h, part in enumerate(one_row(wide, first + r, probe_local, rows)):
                out_ref[r, :probe_local, h * BLK : (h + 1) * BLK] = part.astype(BF16)
            whole = kappa_ref[first + r : first + r + 1, :]
            high = whole.astype(BF16).astype(F32)
            rest = whole - high
            middle = rest.astype(BF16).astype(F32)
            low = rest - middle
            pieces = jnp.where(place == 0, high, jnp.where(place == 1, middle, jnp.where(place == 2, low, 0.0)))
            out_ref[r, probe_local:, :] = pieces.astype(BF16)


def kappa_rows(kappa_ref, above_ref, below_ref, probe_local):
    def halo(ref, r):
        piece = ref[r, probe_local:, :].astype(F32)
        return piece[0:1] + piece[1:2] + piece[2:3]

    rows = kappa_ref.shape[0]
    return (
        [halo(above_ref, r) for r in range(SMOOTH)]
        + [kappa_ref[r : r + 1, :] for r in range(rows)]
        + [halo(below_ref, r) for r in range(SMOOTH)]
    )


def put_row(ref, blk, at, row):
    for h, part in enumerate(row):
        ref[blk + h, at, :] = part


def smooth_step(f, coef, lane, r):
    lap = around(f[r - 1], f[r], f[r + 1], lane)
    return [x + coef[r, :, h * BLK : (h + 1) * BLK] * y for h, (x, y) in enumerate(zip(f[r], lap))]


def coefficients(coef, kappas):
    for r, k in kappas:
        coef[r] = jnp.broadcast_to(k, coef.shape[1:])


def lanes():
    return lax.broadcasted_iota(jnp.int32, (SUB, BLK), 1)


def keep_state(state_ref, step, f, at):
    rows = len(f)
    for side, first in ((0, step), (1, rows - 2 - step)):
        for i in range(2):
            for h, part in enumerate(f[first + i]):
                state_ref[side, step, i, at, h * BLK : (h + 1) * BLK] = part


def outer_rows(kappas):
    total, reach = len(kappas), 2 * SMOOTH + 1
    return [(r, k) for r, k in enumerate(kappas) if r < reach or r >= total - reach]


def smooth_inner_kernel(probes_ref, kappa_ref, field_ref, state_ref, wide, coef, result):
    rows, lon = kappa_ref.shape
    probe_local = probes_ref.shape[0] // rows
    halves = lon // BLK
    widen(probes_ref, wide)
    coefficients(coef, [(r, kappa_ref[r : r + 1, :]) for r in range(rows)])
    lane = lanes()

    @pl.loop(0, probe_local // SUB, unroll=2)
    def _(c):
        base = pl.multiple_of(c * SUB, SUB)
        at = pl.ds(base, SUB)
        f = [one_row(wide, base * rows + r, SUB, rows) for r in range(rows)]
        for step in range(SMOOTH):
            keep_state(state_ref, step, f, at)
            f = [smooth_step(f, coef, lane, r) if step < r < rows - 1 - step else f[r] for r in range(rows)]
        for r in range(SMOOTH, rows - SMOOTH):
            put_row(result, (r - SMOOTH) * halves, at, f[r])

    field_ref[...] = result[...].astype(BF16)


def side_rows(state_ref, side, step, mine, at):
    inner = [split_row(state_ref[side, step, i, at, :]) for i in range(2)]
    return mine + inner if side == 0 else inner + mine


def smooth_outer_kernel(kappa_ref, above_ref, below_ref, state_ref, field_ref, coef, halos, result):
    rows, lon = kappa_ref.shape
    probe_local = state_ref.shape[3]
    halves = lon // BLK
    halos[0] = above_ref[:, :probe_local, :].astype(F32)
    halos[1] = below_ref[:, :probe_local, :].astype(F32)
    coefficients(coef, outer_rows(kappa_rows(kappa_ref, above_ref, below_ref, probe_local)))
    lane = lanes()
    total = rows + 2 * SMOOTH

    @pl.loop(0, probe_local // SUB, unroll=2)
    def _(c):
        base = pl.multiple_of(c * SUB, SUB)
        at = pl.ds(base, SUB)
        for side in range(2):
            mine = [split_row(halos[side, r, at, :]) for r in range(SMOOTH)]
            for step in range(SMOOTH):
                f = side_rows(state_ref, side, step, mine, at)
                first = step if side == 0 else total - 6 - step
                rows_at = dict(enumerate(f, first))
                new = range(first + 1, first + 5)
                mine = [smooth_step(rows_at, coef, lane, r) for r in new]
            for r in range(SMOOTH):
                put_row(result, (side * SMOOTH + r) * halves, at, mine[r])

    field_ref[...] = result[...].astype(BF16)


def hold_kernel(blocks_ref, after_ref, held_ref, arrived):
    copy = pltpu.make_async_copy(blocks_ref, held_ref, arrived)
    copy.start()
    copy.wait()


def each_slot(slots, body):
    @pl.loop(0, slots // GROUP)
    def _(g):
        for i in range(GROUP):
            body(g * GROUP + i)


def forward_kernel(
    sources,
    receptors,
    count,
    place,
    blocks_ref,
    near_in,
    near_out,
    far_in,
    far_out,
    keep_ref,
    give_ref,
    turned,
    total,
    held,
    arrived,
):
    fetches = []
    size = held.shape[0] // FETCHES
    for g in range(FETCHES):
        at = pl.ds(g * size, size)
        fetches.append(pltpu.make_async_copy(blocks_ref.at[at], held.at[at], arrived.at[g]))
        fetches[g].start()
    total[...] = jnp.zeros_like(total)
    edge = near_out.shape[0] // 2
    for j in range(turned.shape[0]):
        if edge <= j < turned.shape[0] - edge:
            near, far = near_in[j - edge], far_in[j - edge]
        else:
            at = j if j < edge else j - near_in.shape[0]
            near, far = near_out[at], far_out[at]
        turned[j] = jnp.concatenate([near, far], axis=0).T

    spare = total.shape[0] - 1

    def slot(n):
        b = jnp.where(n < count[0], receptors[n], spare)
        total[b] += jnp.dot(held[n], turned[sources[n]], preferred_element_type=F32)

    for g, fetch in enumerate(fetches):
        fetch.wait()
        for i in range(size):
            slot(g * size + i)
    half = keep_ref.shape[0]
    for out_ref, side in ((keep_ref, place[0]), (give_ref, 1 - place[0])):
        for b in range(half):
            out_ref[b] = total[side * half + b].T.astype(BF16)


def adjoint_kernel(
    sources, receptors, count, place, held, mine_ref, theirs_ref, near_in, near_out, far_in, far_out, weighted, total
):
    total[...] = jnp.zeros_like(total)
    pieces, share = mine_ref.shape[:2]
    for side_ref, side in ((mine_ref, place[0]), (theirs_ref, 1 - place[0])):
        for k in range(pieces):
            row = (side * pieces + lax.bitwise_xor(place[1], k)) * share
            weighted[pl.ds(pl.multiple_of(row, share), share), :] = side_ref[k]

    spare = total.shape[0] - 1
    pair = total.shape[1]

    def slot(n):
        j = jnp.where(n < count[0], sources[n], spare)
        entries = weighted[pl.ds(pl.multiple_of(receptors[n] * pair, pair), pair), :]
        total[j] += jnp.dot(entries, held[n], preferred_element_type=F32)

    each_slot(held.shape[0], slot)
    half = near_in.shape[1]
    edge = near_out.shape[0] // 2
    for at, in_ref, out_ref in ((pl.ds(0, half), near_in, near_out), (pl.ds(half, half), far_in, far_out)):
        out_ref[:edge] = total[:edge, at].astype(BF16)
        in_ref[...] = total[edge : spare - edge, at].astype(BF16)
        out_ref[edge:] = total[spare - edge : spare, at].astype(BF16)


def block_row(ref, first, at, halves):
    return [ref[first + h, at, :] for h in range(halves)]


def times_kappa(coef, f, r):
    return [coef[r, :, h * BLK : (h + 1) * BLK] * x for h, x in enumerate(f[r])]


def back_inner_kernel(
    probes_ref, kappa_ref, own_in, core_in, far_in, own_out, core_out, far_out, wide, state_ref, coef, terms
):
    rows, lon = kappa_ref.shape
    probe_local = probes_ref.shape[0] // rows
    halves = lon // BLK
    edge = own_out.shape[0] // 2
    widen(probes_ref, wide)
    inner = own_in[...].astype(F32) + core_in[...].astype(F32) + far_in[...].astype(F32)
    outer = own_out[...].astype(F32) + core_out[...].astype(F32) + far_out[...].astype(F32)
    terms[:edge] = outer[:edge]
    terms[edge : terms.shape[0] - edge] = inner
    terms[terms.shape[0] - edge :] = outer[edge:]
    lane = lanes()
    coefficients(coef, [(r, kappa_ref[r : r + 1, :]) for r in range(rows)])

    @pl.loop(0, probe_local // SUB, unroll=2)
    def _(c):
        base = pl.multiple_of(c * SUB, SUB)
        at = pl.ds(base, SUB)
        f = [block_row(terms, r * halves, at, halves) for r in range(rows)]
        for step in range(SMOOTH):
            keep_state(state_ref, step, f, at)
            g = {r: times_kappa(coef, f, r) for r in (step, step + 1)}
            new = list(f)
            for r in range(step + 1, rows - 1 - step):
                g[r + 1] = times_kappa(coef, f, r + 1)
                new[r] = [x + y for x, y in zip(f[r], around(g[r - 1], g[r], g[r + 1], lane))]
            f = new
        for r in range(SMOOTH, rows - SMOOTH):
            for h in range(halves):
                wide[h, pl.ds(base * rows + r, SUB, stride=rows), :] += f[r][h]


def back_outer_kernel(
    inside, kappa_ref, above_ref, below_ref, top_ref, bottom_ref, state_ref, done_ref, out_hbm, wide, coef, halos, sent
):
    rows, lon = kappa_ref.shape
    probe_local = state_ref.shape[3]
    halves = lon // BLK
    total = rows + 2 * SMOOTH
    halos[0] = top_ref[...].astype(F32)
    halos[1] = bottom_ref[...].astype(F32)
    lane = lanes()
    coefficients(coef, outer_rows(kappa_rows(kappa_ref, above_ref, below_ref, probe_local)))

    def sends(c):
        lines = pl.ds(pl.multiple_of(c * SUB * rows, SUB * rows), SUB * rows)
        return [
            pltpu.make_async_copy(wide.at[h, lines], out_hbm.at[lines, h * BLK : (h + 1) * BLK], sent.at[c, h])
            for h in range(halves)
        ]

    @pl.loop(0, probe_local // SUB, unroll=2)
    def _(c):
        base = pl.multiple_of(c * SUB, SUB)
        at = pl.ds(base, SUB)
        lines = pl.ds(pl.multiple_of(base * rows, SUB * rows), SUB * rows)
        wide[:, lines, :] = done_ref[:, lines, :]
        for side in range(2):
            mine = [block_row(halos.at[side], r * halves, at, halves) for r in range(SMOOTH)]
            for step in range(SMOOTH):
                first = step if side == 0 else total - 6 - step
                f = dict(enumerate(side_rows(state_ref, side, step, mine, at), first))
                g = {r: times_kappa(coef, f, r) for r in f}
                mine = []
                for r in range(first + 1, first + 5):
                    lap = around(g[r - 1], g[r], g[r + 1], lane)
                    if not SMOOTH <= r < total - SMOOTH:
                        lap = [x * inside[side] for x in lap]
                    mine.append([x + y for x, y in zip(f[r], lap)])
            for r in range(SMOOTH):
                row = r if side == 0 else rows - SMOOTH + r
                for h in range(halves):
                    wide[h, pl.ds(base * rows + row, SUB, stride=rows), :] += mine[r][h]
        for copy in sends(c):
            copy.start()

    for c in range(probe_local // SUB):
        for copy in sends(c):
            copy.wait()


def swap(x, axis, distance):
    size = lax.axis_size(axis)
    return lax.ppermute(x, axis, [(i, i ^ distance) for i in range(size)])


def far_first(size):
    return sorted(range(1, size), key=lambda k: -k.bit_length())


def exchange_edges(north, south):
    size = lax.axis_size("src")
    down = [(i, i + 1) for i in range(size - 1)]
    up = [(j, i) for i, j in down]
    return lax.ppermute(south, "src", down), lax.ppermute(north, "src", up)


def per_device(probes, kappa, footprint, block_source, block_receptor, block_count, obs_weight):
    probe_local, rows, lon = probes.shape
    halves = lon // BLK
    cells = rows * halves
    tiles = lax.axis_size("src")
    me = lax.axis_index("src")
    blocks = footprint.reshape(footprint.shape[2:])
    slots = blocks.shape[0]
    flat = probes.reshape(probe_local * rows, lon)
    pair = 2 * probe_local

    edge = jax.ShapeDtypeStruct((SMOOTH, probe_local + PIECES, lon), BF16)
    north, south, flat, kappa = pl.pallas_call(
        edge_kernel,
        out_shape=(edge, edge, jax.ShapeDtypeStruct(flat.shape, BF16), jax.ShapeDtypeStruct(kappa.shape, F32)),
        in_specs=[HBM, HBM],
        out_specs=(VMEM,) * 4,
        scratch_shapes=[
            pltpu.VMEM((halves, probe_local * rows, BLK), F32),
            pltpu.SemaphoreType.DMA((2,)),
        ],
        compiler_params=params(),
        name="edges",
    )(in_hbm(flat), in_hbm(kappa))
    above, below = exchange_edges(north, south)

    def hold(after):
        return pl.pallas_call(
            hold_kernel,
            out_shape=jax.ShapeDtypeStruct(blocks.shape, BF16),
            in_specs=[HBM, pl.BlockSpec(memory_space=pl.ANY)],
            out_specs=VMEM,
            scratch_shapes=[pltpu.SemaphoreType.DMA],
            compiler_params=params(),
            cost_estimate=pl.CostEstimate(flops=0, bytes_accessed=4 * slots * BLK * BLK, transcendentals=0),
            name="hold",
        )(in_hbm(blocks), after)

    edge_cells = SMOOTH * halves
    inner_part = jax.ShapeDtypeStruct((cells - 2 * edge_cells, probe_local, BLK), BF16)
    outer_part = jax.ShapeDtypeStruct((2 * edge_cells, probe_local, BLK), BF16)
    state = jax.ShapeDtypeStruct((2, SMOOTH, 2, probe_local, lon), F32)
    by_half = (halves, probe_local * rows, BLK)
    halo_rows = rows + 2 * SMOOTH
    own_in, smooth_state = pl.pallas_call(
        smooth_inner_kernel,
        out_shape=(inner_part, state),
        in_specs=[VMEM] * 2,
        out_specs=(VMEM, VMEM),
        scratch_shapes=[
            pltpu.VMEM(by_half, F32),
            pltpu.VMEM((rows, SUB, lon), F32),
            pltpu.VMEM(inner_part.shape, F32),
        ],
        compiler_params=params(),
        name="smooth_inner",
    )(flat, kappa)
    own_out = pl.pallas_call(
        smooth_outer_kernel,
        out_shape=outer_part,
        in_specs=[VMEM] * 4,
        out_specs=VMEM,
        scratch_shapes=[
            pltpu.VMEM((halo_rows, SUB, lon), F32),
            pltpu.VMEM((2, SMOOTH, probe_local, lon), F32),
            pltpu.VMEM(outer_part.shape, F32),
        ],
        compiler_params=params(),
        name="smooth_outer",
    )(kappa, above, below, smooth_state)

    side, row = me % 2, me // 2
    place = jnp.stack([side, row]).astype(jnp.int32)
    scalars = (block_source.reshape(-1), block_receptor.reshape(-1), block_count.reshape(-1), place)
    spread_over = tiles // 2
    share = RB_LOC * pair // tiles

    def over_slots(kernel, footprints, footprints_spec, operands, outs, scratch):
        return pl.pallas_call(
            kernel,
            out_shape=outs,
            in_specs=[SMEM] * len(scalars) + [footprints_spec] + [VMEM] * len(operands),
            out_specs=jax.tree.map(lambda _: VMEM, outs),
            scratch_shapes=scratch,
            compiler_params=params(),
            cost_estimate=pl.CostEstimate(
                flops=2 * slots * BLK * BLK * pair, bytes_accessed=2 * slots * BLK * BLK, transcendentals=0
            ),
            name=kernel.__name__,
        )(*scalars, footprints, *operands)

    def forward(*fields):
        half = jax.ShapeDtypeStruct((RB_LOC // 2, pair, BLK), BF16)
        return over_slots(
            forward_kernel,
            in_hbm(blocks),
            HBM,
            fields,
            (half, half),
            [
                pltpu.VMEM((cells, BLK, pair), BF16),
                pltpu.VMEM((RB_LOC + 1, BLK, pair), F32),
                pltpu.VMEM(blocks.shape, BF16),
                pltpu.SemaphoreType.DMA((FETCHES,)),
            ],
        )

    def adjoint(held, mine, theirs):
        return over_slots(
            adjoint_kernel,
            held,
            VMEM,
            (mine, theirs),
            (inner_part, outer_part) * 2,
            [pltpu.VMEM((RB_LOC * pair, BLK), BF16), pltpu.VMEM((cells + 1, pair, BLK), F32)],
        )

    first_row = (side * spread_over + row) * share
    held_blocks = max(share // pair, 1)
    weights = lax.dynamic_slice_in_dim(obs_weight.reshape(RB_LOC, 1, BLK), first_row // pair, held_blocks)
    weights = jnp.broadcast_to(weights, (held_blocks, share // held_blocks, BLK)).reshape(share, BLK)

    def summed(keep, give):
        got = swap(give, "src", 1)
        pairs = (keep.astype(F32) + got.astype(F32)).astype(BF16).reshape(spread_over, share, BLK)
        picked = lambda k: lax.dynamic_index_in_dim(pairs, lax.bitwise_xor(row, k), 0, False)
        total = picked(0).astype(F32)
        for k in far_first(spread_over):
            total = total + swap(picked(k), "src", 2 * k).astype(F32)
        return (weights * total).astype(BF16)

    def gathered(weighted):
        pieces = {k: swap(weighted, "src", 2 * k) for k in far_first(spread_over)}
        return jnp.stack([weighted] + [pieces[k] for k in range(1, spread_over)])

    def spread(weighted):
        mine = gathered(weighted)
        return mine, swap(mine, "src", 1)

    own = (own_in, own_out)
    other = [swap(x, "rcv", 2) for x in own]
    beside = [swap(x, "rcv", 1) for x in own]
    near_keep, near_give = forward(*own, *beside)
    other[1], near_give = lax.optimization_barrier((other[1], near_give))
    first = summed(near_keep, near_give)
    second = summed(*forward(*other, *[swap(x, "rcv", 1) for x in other]))

    held = hold(first)
    first_mine = gathered(first)
    second_mine = gathered(second)
    second_mine, _ = lax.optimization_barrier((second_mine, first_mine))
    mine_in, mine_out, *to_beside = adjoint(held, first_mine, swap(first_mine, "src", 1))
    beside_in, beside_out = [swap(x, "rcv", 1) for x in to_beside]
    second_halves = (second_mine, swap(second_mine, "src", 1))
    second_halves, mine_in = lax.optimization_barrier((second_halves, mine_in))
    other_in, other_out, diagonal_in, diagonal_out = adjoint(held, *second_halves)
    both = lambda here, there: (here.astype(F32) + swap(there, "rcv", 1).astype(F32)).astype(BF16)
    far_out = swap(both(other_out, diagonal_out), "rcv", 2)
    far_in = swap(both(other_in, diagonal_in), "rcv", 2)

    edges = (mine_out.astype(F32) + beside_out.astype(F32) + far_out.astype(F32)).astype(BF16)
    top, bottom = exchange_edges(edges[:edge_cells], edges[edge_cells:])
    inside = jnp.stack([me > 0, me < tiles - 1]).astype(F32)
    inner, back_state = pl.pallas_call(
        back_inner_kernel,
        out_shape=(jax.ShapeDtypeStruct(by_half, F32), state),
        in_specs=[VMEM] * 8,
        out_specs=(VMEM, VMEM),
        scratch_shapes=[pltpu.VMEM((rows, SUB, lon), F32), pltpu.VMEM((cells, probe_local, BLK), F32)],
        compiler_params=params(),
        name="back_inner",
    )(flat, kappa, mine_in, beside_in, far_in, mine_out, beside_out, far_out)
    out = pl.pallas_call(
        back_outer_kernel,
        out_shape=jax.ShapeDtypeStruct((probe_local * rows, lon), F32),
        in_specs=[SMEM] + [VMEM] * 7,
        out_specs=HBM,
        scratch_shapes=[
            pltpu.VMEM(by_half, F32),
            pltpu.VMEM((halo_rows, SUB, lon), F32),
            pltpu.VMEM((2, edge_cells, probe_local, BLK), F32),
            pltpu.SemaphoreType.DMA((probe_local // SUB, halves)),
        ],
        compiler_params=params(),
        name="back_outer",
    )(inside, kappa, above, below, top, bottom, back_state, inner)
    return out.reshape(probe_local, rows, lon)


def solution(mesh):
    placed = (
        P("rcv", "src", None),
        P("src", None),
        P("src", "rcv", None, None, None),
        P("src", "rcv", None),
        P("src", "rcv", None),
        P("src", "rcv"),
        P("rcv"),
    )
    return jax.shard_map(
        per_device, mesh=mesh, in_specs=placed, out_specs=P("rcv", "src", None), check_vma=False
    )
```

```python
import jax
import jax.numpy as jnp
from jax import lax
from jax.experimental import pallas as pl
from jax.experimental.pallas import tpu as pltpu
from jax.sharding import PartitionSpec as P

BLK = 128
RB_LOC = 16
SMOOTH = 4
SUB = 8
PIECES = 16
GROUP = 32
FETCHES = 4
F32, BF16 = jnp.float32, jnp.bfloat16
VMEM = pl.BlockSpec(memory_space=pltpu.VMEM)
SMEM = pl.BlockSpec(memory_space=pltpu.SMEM)
HBM = pl.BlockSpec(memory_space=pltpu.HBM)


def in_hbm(x):
    return pltpu.with_memory_space_constraint(x, pltpu.HBM)


def params(mib=24):
    return pltpu.CompilerParams(vmem_limit_bytes=mib * 1024 * 1024)


def widen(probes_ref, wide):
    for h in range(wide.shape[0]):
        wide[h] = probes_ref[:, h * BLK : (h + 1) * BLK].astype(F32)


def one_row(wide, start, size, rows):
    at = pl.ds(start, size, stride=rows)
    return [wide[h, at, :] for h in range(wide.shape[0])]


def split_row(row):
    return [row[:, h * BLK : (h + 1) * BLK] for h in range(row.shape[1] // BLK)]


def around(north, row, south, lane):
    east = [pltpu.roll(x, 1, 1) for x in row]
    west = [pltpu.roll(x, BLK - 1, 1) for x in row]
    out = []
    for h, x in enumerate(row):
        left = jnp.where(lane > 0, east[h], east[h - 1] if h else 0.0)
        right = jnp.where(lane < BLK - 1, west[h], west[h + 1] if h + 1 < len(row) else 0.0)
        out.append(((north[h] + south[h]) + (left + right)) - 4.0 * x)
    return out


def edge_kernel(probes_hbm, kappa_hbm, north_ref, south_ref, probes_ref, kappa_ref, wide, arrived):
    fetches = [
        pltpu.make_async_copy(probes_hbm, probes_ref, arrived.at[0]),
        pltpu.make_async_copy(kappa_hbm, kappa_ref, arrived.at[1]),
    ]
    for fetch in fetches:
        fetch.start()
    for fetch in fetches:
        fetch.wait()
    rows, lon = kappa_ref.shape
    probe_local = probes_ref.shape[0] // rows
    widen(probes_ref, wide)
    place = lax.broadcasted_iota(jnp.int32, (PIECES, lon), 0)
    for out_ref, first in ((north_ref, 0), (south_ref, rows - SMOOTH)):
        pieces = jnp.zeros((PIECES, lon), F32)
        for r in range(SMOOTH):
            for h, part in enumerate(one_row(wide, first + r, probe_local, rows)):
                out_ref[r * probe_local : (r + 1) * probe_local, h * BLK : (h + 1) * BLK] = part.astype(BF16)
            whole = kappa_ref[first + r : first + r + 1, :]
            high = whole.astype(BF16).astype(F32)
            rest = whole - high
            middle = rest.astype(BF16).astype(F32)
            for i, piece in enumerate((high, middle, rest - middle)):
                pieces = jnp.where(place == i * SMOOTH + r, piece, pieces)
        out_ref[SMOOTH * probe_local :, :] = pieces.astype(BF16)


def kappa_rows(kappa_ref, above_ref, below_ref, probe_local):
    def halo(ref, r):
        pieces = ref[SMOOTH * probe_local :, :].astype(F32)
        high, middle, low = [pieces[i * SMOOTH + r : i * SMOOTH + r + 1] for i in range(3)]
        return high + middle + low

    rows = kappa_ref.shape[0]
    return (
        [halo(above_ref, r) for r in range(SMOOTH)]
        + [kappa_ref[r : r + 1, :] for r in range(rows)]
        + [halo(below_ref, r) for r in range(SMOOTH)]
    )


def put_row(ref, blk, at, row):
    for h, part in enumerate(row):
        ref[blk + h, at, :] = part


def smooth_step(f, coef, lane, r):
    lap = around(f[r - 1], f[r], f[r + 1], lane)
    return [x + coef[r, :, h * BLK : (h + 1) * BLK] * y for h, (x, y) in enumerate(zip(f[r], lap))]


def coefficients(coef, kappas):
    for r, k in kappas:
        coef[r] = jnp.broadcast_to(k, coef.shape[1:])


def lanes():
    return lax.broadcasted_iota(jnp.int32, (SUB, BLK), 1)


def keep_state(state_ref, step, f, at):
    rows = len(f)
    for side, first in ((0, step), (1, rows - 2 - step)):
        for i in range(2):
            for h, part in enumerate(f[first + i]):
                state_ref[side, step, i, at, h * BLK : (h + 1) * BLK] = part


def outer_rows(kappas):
    total, reach = len(kappas), 2 * SMOOTH + 1
    return [(r, k) for r, k in enumerate(kappas) if r < reach or r >= total - reach]


def smooth_inner_kernel(probes_ref, kappa_ref, field_ref, state_ref, wide, coef, result):
    rows, lon = kappa_ref.shape
    probe_local = probes_ref.shape[0] // rows
    halves = lon // BLK
    widen(probes_ref, wide)
    coefficients(coef, [(r, kappa_ref[r : r + 1, :]) for r in range(rows)])
    lane = lanes()

    @pl.loop(0, probe_local // SUB, unroll=2)
    def _(c):
        base = pl.multiple_of(c * SUB, SUB)
        at = pl.ds(base, SUB)
        f = [one_row(wide, base * rows + r, SUB, rows) for r in range(rows)]
        for step in range(SMOOTH):
            keep_state(state_ref, step, f, at)
            f = [smooth_step(f, coef, lane, r) if step < r < rows - 1 - step else f[r] for r in range(rows)]
        for r in range(SMOOTH, rows - SMOOTH):
            put_row(result, (r - SMOOTH) * halves, at, f[r])

    field_ref[...] = result[...].astype(BF16)


def side_rows(state_ref, side, step, mine, at):
    inner = [split_row(state_ref[side, step, i, at, :]) for i in range(2)]
    return mine + inner if side == 0 else inner + mine


def smooth_outer_kernel(kappa_ref, above_ref, below_ref, state_ref, field_ref, coef, halos, result):
    rows, lon = kappa_ref.shape
    probe_local = state_ref.shape[3]
    halves = lon // BLK
    for r in range(SMOOTH):
        halos[0, r] = above_ref[r * probe_local : (r + 1) * probe_local, :].astype(F32)
        halos[1, r] = below_ref[r * probe_local : (r + 1) * probe_local, :].astype(F32)
    coefficients(coef, outer_rows(kappa_rows(kappa_ref, above_ref, below_ref, probe_local)))
    lane = lanes()
    total = rows + 2 * SMOOTH

    @pl.loop(0, probe_local // SUB, unroll=2)
    def _(c):
        base = pl.multiple_of(c * SUB, SUB)
        at = pl.ds(base, SUB)
        for side in range(2):
            mine = [split_row(halos[side, r, at, :]) for r in range(SMOOTH)]
            for step in range(SMOOTH):
                f = side_rows(state_ref, side, step, mine, at)
                first = step if side == 0 else total - 6 - step
                rows_at = dict(enumerate(f, first))
                new = range(first + 1, first + 5)
                mine = [smooth_step(rows_at, coef, lane, r) for r in new]
            for r in range(SMOOTH):
                put_row(result, (side * SMOOTH + r) * halves, at, mine[r])

    field_ref[...] = result[...].astype(BF16)


def hold_kernel(blocks_ref, after_ref, held_ref, arrived):
    copy = pltpu.make_async_copy(blocks_ref, held_ref, arrived)
    copy.start()
    copy.wait()


def each_slot(slots, body):
    @pl.loop(0, slots // GROUP)
    def _(g):
        for i in range(GROUP):
            body(g * GROUP + i)


def forward_kernel(
    sources_hbm,
    receptors_hbm,
    count,
    place,
    blocks_ref,
    near_in,
    near_out,
    far_in,
    far_out,
    keep_ref,
    give_ref,
    turned,
    total,
    held,
    arrived,
    sources,
    receptors,
    listed,
):
    lists = [
        pltpu.make_async_copy(sources_hbm, sources, listed.at[0]),
        pltpu.make_async_copy(receptors_hbm, receptors, listed.at[1]),
    ]
    for fetch in lists:
        fetch.start()
    fetches = []
    size = held.shape[0] // FETCHES
    for g in range(FETCHES):
        at = pl.ds(g * size, size)
        fetches.append(pltpu.make_async_copy(blocks_ref.at[at], held.at[at], arrived.at[g]))
        fetches[g].start()
    total[...] = jnp.zeros_like(total)
    edge = near_out.shape[0] // 2
    for j in range(turned.shape[0]):
        if edge <= j < turned.shape[0] - edge:
            near, far = near_in[j - edge], far_in[j - edge]
        else:
            at = j if j < edge else j - near_in.shape[0]
            near, far = near_out[at], far_out[at]
        turned[j] = jnp.concatenate([near, far], axis=0).T

    spare = total.shape[0] - 1

    def slot(n):
        b = jnp.where(n < count[0], receptors[n], spare)
        total[b] += jnp.dot(held[n], turned[sources[n]], preferred_element_type=F32)

    for fetch in lists:
        fetch.wait()
    for g, fetch in enumerate(fetches):
        fetch.wait()
        for i in range(size):
            slot(g * size + i)
    half = keep_ref.shape[0]
    for out_ref, side in ((keep_ref, place[0]), (give_ref, 1 - place[0])):
        for b in range(half):
            out_ref[b] = total[side * half + b].T.astype(BF16)


def adjoint_kernel(
    sources, receptors, count, place, held, mine_ref, theirs_ref, near_in, near_out, far_in, far_out, weighted, total
):
    total[...] = jnp.zeros_like(total)
    pieces, share = mine_ref.shape[:2]
    for side_ref, side in ((mine_ref, place[0]), (theirs_ref, 1 - place[0])):
        for k in range(pieces):
            row = (side * pieces + lax.bitwise_xor(place[1], k)) * share
            weighted[pl.ds(pl.multiple_of(row, share), share), :] = side_ref[k]

    spare = total.shape[0] - 1
    pair = total.shape[1]

    def slot(n):
        j = jnp.where(n < count[0], sources[n], spare)
        entries = weighted[pl.ds(pl.multiple_of(receptors[n] * pair, pair), pair), :]
        total[j] += jnp.dot(entries, held[n], preferred_element_type=F32)

    each_slot(held.shape[0], slot)
    half = near_in.shape[1]
    edge = near_out.shape[0] // 2
    for at, in_ref, out_ref in ((pl.ds(0, half), near_in, near_out), (pl.ds(half, half), far_in, far_out)):
        out_ref[:edge] = total[:edge, at].astype(BF16)
        in_ref[...] = total[edge : spare - edge, at].astype(BF16)
        out_ref[edge:] = total[spare - edge : spare, at].astype(BF16)


def block_row(ref, first, at, halves):
    return [ref[first + h, at, :] for h in range(halves)]


def times_kappa(coef, f, r):
    return [coef[r, :, h * BLK : (h + 1) * BLK] * x for h, x in enumerate(f[r])]


def back_inner_kernel(
    probes_ref, kappa_ref, own_in, core_in, far_in, own_out, core_out, far_out, wide, state_ref, coef, terms
):
    rows, lon = kappa_ref.shape
    probe_local = probes_ref.shape[0] // rows
    halves = lon // BLK
    edge = own_out.shape[0] // 2
    widen(probes_ref, wide)
    inner = own_in[...].astype(F32) + core_in[...].astype(F32) + far_in[...].astype(F32)
    outer = own_out[...].astype(F32) + core_out[...].astype(F32) + far_out[...].astype(F32)
    terms[:edge] = outer[:edge]
    terms[edge : terms.shape[0] - edge] = inner
    terms[terms.shape[0] - edge :] = outer[edge:]
    lane = lanes()
    coefficients(coef, [(r, kappa_ref[r : r + 1, :]) for r in range(rows)])

    @pl.loop(0, probe_local // SUB, unroll=2)
    def _(c):
        base = pl.multiple_of(c * SUB, SUB)
        at = pl.ds(base, SUB)
        f = [block_row(terms, r * halves, at, halves) for r in range(rows)]
        for step in range(SMOOTH):
            keep_state(state_ref, step, f, at)
            g = {r: times_kappa(coef, f, r) for r in (step, step + 1)}
            new = list(f)
            for r in range(step + 1, rows - 1 - step):
                g[r + 1] = times_kappa(coef, f, r + 1)
                new[r] = [x + y for x, y in zip(f[r], around(g[r - 1], g[r], g[r + 1], lane))]
            f = new
        for r in range(SMOOTH, rows - SMOOTH):
            for h in range(halves):
                wide[h, pl.ds(base * rows + r, SUB, stride=rows), :] += f[r][h]


def back_outer_kernel(
    inside, kappa_ref, above_ref, below_ref, top_ref, bottom_ref, state_ref, done_ref, out_hbm, wide, coef, halos, sent
):
    rows, lon = kappa_ref.shape
    probe_local = state_ref.shape[3]
    halves = lon // BLK
    total = rows + 2 * SMOOTH
    halos[0] = top_ref[...].astype(F32)
    halos[1] = bottom_ref[...].astype(F32)
    lane = lanes()
    coefficients(coef, outer_rows(kappa_rows(kappa_ref, above_ref, below_ref, probe_local)))

    def sends(c):
        lines = pl.ds(pl.multiple_of(c * SUB * rows, SUB * rows), SUB * rows)
        return [
            pltpu.make_async_copy(wide.at[h, lines], out_hbm.at[lines, h * BLK : (h + 1) * BLK], sent.at[c, h])
            for h in range(halves)
        ]

    @pl.loop(0, probe_local // SUB, unroll=2)
    def _(c):
        base = pl.multiple_of(c * SUB, SUB)
        at = pl.ds(base, SUB)
        lines = pl.ds(pl.multiple_of(base * rows, SUB * rows), SUB * rows)
        wide[:, lines, :] = done_ref[:, lines, :]
        for side in range(2):
            mine = [block_row(halos.at[side], r * halves, at, halves) for r in range(SMOOTH)]
            for step in range(SMOOTH):
                first = step if side == 0 else total - 6 - step
                f = dict(enumerate(side_rows(state_ref, side, step, mine, at), first))
                g = {r: times_kappa(coef, f, r) for r in f}
                mine = []
                for r in range(first + 1, first + 5):
                    lap = around(g[r - 1], g[r], g[r + 1], lane)
                    if not SMOOTH <= r < total - SMOOTH:
                        lap = [x * inside[side] for x in lap]
                    mine.append([x + y for x, y in zip(f[r], lap)])
            for r in range(SMOOTH):
                row = r if side == 0 else rows - SMOOTH + r
                for h in range(halves):
                    wide[h, pl.ds(base * rows + row, SUB, stride=rows), :] += mine[r][h]
        for copy in sends(c):
            copy.start()

    for c in range(probe_local // SUB):
        for copy in sends(c):
            copy.wait()


def swap(x, axis, distance):
    size = lax.axis_size(axis)
    return lax.ppermute(x, axis, [(i, i ^ distance) for i in range(size)])


def far_first(size):
    return sorted(range(1, size), key=lambda k: -k.bit_length())


def exchange_edges(north, south):
    size = lax.axis_size("src")
    down = [(i, i + 1) for i in range(size - 1)]
    up = [(j, i) for i, j in down]
    return lax.ppermute(south, "src", down), lax.ppermute(north, "src", up)


def per_device(probes, kappa, footprint, block_source, block_receptor, block_count, obs_weight):
    probe_local, rows, lon = probes.shape
    halves = lon // BLK
    cells = rows * halves
    tiles = lax.axis_size("src")
    me = lax.axis_index("src")
    blocks = footprint.reshape(footprint.shape[2:])
    slots = blocks.shape[0]
    flat = probes.reshape(probe_local * rows, lon)
    pair = 2 * probe_local

    edge = jax.ShapeDtypeStruct((SMOOTH * probe_local + PIECES, lon), BF16)
    north, south, flat, kappa = pl.pallas_call(
        edge_kernel,
        out_shape=(edge, edge, jax.ShapeDtypeStruct(flat.shape, BF16), jax.ShapeDtypeStruct(kappa.shape, F32)),
        in_specs=[HBM, HBM],
        out_specs=(VMEM,) * 4,
        scratch_shapes=[
            pltpu.VMEM((halves, probe_local * rows, BLK), F32),
            pltpu.SemaphoreType.DMA((2,)),
        ],
        compiler_params=params(),
        name="edges",
    )(in_hbm(flat), in_hbm(kappa))
    above, below = exchange_edges(north, south)

    def hold(after):
        return pl.pallas_call(
            hold_kernel,
            out_shape=jax.ShapeDtypeStruct(blocks.shape, BF16),
            in_specs=[HBM, pl.BlockSpec(memory_space=pl.ANY)],
            out_specs=VMEM,
            scratch_shapes=[pltpu.SemaphoreType.DMA],
            compiler_params=params(),
            cost_estimate=pl.CostEstimate(flops=0, bytes_accessed=4 * slots * BLK * BLK, transcendentals=0),
            name="hold",
        )(in_hbm(blocks), after)

    edge_cells = SMOOTH * halves
    inner_part = jax.ShapeDtypeStruct((cells - 2 * edge_cells, probe_local, BLK), BF16)
    outer_part = jax.ShapeDtypeStruct((2 * edge_cells, probe_local, BLK), BF16)
    state = jax.ShapeDtypeStruct((2, SMOOTH, 2, probe_local, lon), F32)
    by_half = (halves, probe_local * rows, BLK)
    halo_rows = rows + 2 * SMOOTH
    own_in, smooth_state = pl.pallas_call(
        smooth_inner_kernel,
        out_shape=(inner_part, state),
        in_specs=[VMEM] * 2,
        out_specs=(VMEM, VMEM),
        scratch_shapes=[
            pltpu.VMEM(by_half, F32),
            pltpu.VMEM((rows, SUB, lon), F32),
            pltpu.VMEM(inner_part.shape, F32),
        ],
        compiler_params=params(),
        name="smooth_inner",
    )(flat, kappa)
    own_out = pl.pallas_call(
        smooth_outer_kernel,
        out_shape=outer_part,
        in_specs=[VMEM] * 4,
        out_specs=VMEM,
        scratch_shapes=[
            pltpu.VMEM((halo_rows, SUB, lon), F32),
            pltpu.VMEM((2, SMOOTH, probe_local, lon), F32),
            pltpu.VMEM(outer_part.shape, F32),
        ],
        compiler_params=params(),
        name="smooth_outer",
    )(kappa, above, below, smooth_state)

    side, row = me % 2, me // 2
    place = jnp.stack([side, row]).astype(jnp.int32)
    lists = (block_source.reshape(-1), block_receptor.reshape(-1))
    single = (block_count.reshape(-1), place)
    spread_over = tiles // 2
    share = RB_LOC * pair // tiles

    def over_slots(kernel, list_spec, lists, footprints_spec, footprints, operands, outs, scratch):
        return pl.pallas_call(
            kernel,
            out_shape=outs,
            in_specs=[list_spec, list_spec, SMEM, SMEM, footprints_spec] + [VMEM] * len(operands),
            out_specs=jax.tree.map(lambda _: VMEM, outs),
            scratch_shapes=scratch,
            compiler_params=params(),
            cost_estimate=pl.CostEstimate(
                flops=2 * slots * BLK * BLK * pair, bytes_accessed=2 * slots * BLK * BLK, transcendentals=0
            ),
            name=kernel.__name__,
        )(*lists, *single, footprints, *operands)

    def forward(*fields):
        half = jax.ShapeDtypeStruct((RB_LOC // 2, pair, BLK), BF16)
        return over_slots(
            forward_kernel,
            HBM,
            [in_hbm(x) for x in lists],
            HBM,
            in_hbm(blocks),
            fields,
            (half, half),
            [
                pltpu.VMEM((cells, BLK, pair), BF16),
                pltpu.VMEM((RB_LOC + 1, BLK, pair), F32),
                pltpu.VMEM(blocks.shape, BF16),
                pltpu.SemaphoreType.DMA((FETCHES,)),
                pltpu.SMEM((slots,), jnp.int32),
                pltpu.SMEM((slots,), jnp.int32),
                pltpu.SemaphoreType.DMA((2,)),
            ],
        )

    def adjoint(held, mine, theirs):
        return over_slots(
            adjoint_kernel,
            SMEM,
            lists,
            VMEM,
            held,
            (mine, theirs),
            (inner_part, outer_part) * 2,
            [pltpu.VMEM((RB_LOC * pair, BLK), BF16), pltpu.VMEM((cells + 1, pair, BLK), F32)],
        )

    first_row = (side * spread_over + row) * share
    held_blocks = max(share // pair, 1)
    weights = lax.dynamic_slice_in_dim(obs_weight.reshape(RB_LOC, 1, BLK), first_row // pair, held_blocks)
    weights = jnp.broadcast_to(weights, (held_blocks, share // held_blocks, BLK)).reshape(share, BLK)

    def summed(keep, give):
        got = swap(give, "src", 1)
        pairs = (keep.astype(F32) + got.astype(F32)).astype(BF16).reshape(spread_over, share, BLK)
        picked = lambda k: lax.dynamic_index_in_dim(pairs, lax.bitwise_xor(row, k), 0, False)
        total = picked(0).astype(F32)
        for k in far_first(spread_over):
            total = total + swap(picked(k), "src", 2 * k).astype(F32)
        return (weights * total).astype(BF16)

    def gathered(weighted):
        pieces = {k: swap(weighted, "src", 2 * k) for k in far_first(spread_over)}
        return jnp.stack([weighted] + [pieces[k] for k in range(1, spread_over)])

    def spread(weighted):
        mine = gathered(weighted)
        return mine, swap(mine, "src", 1)

    own = (own_in, own_out)
    other = [swap(x, "rcv", 2) for x in own]
    beside = [swap(x, "rcv", 1) for x in own]
    near_keep, near_give = forward(*own, *beside)
    other[1], near_give = lax.optimization_barrier((other[1], near_give))
    first = summed(near_keep, near_give)
    second = summed(*forward(*other, *[swap(x, "rcv", 1) for x in other]))

    held = hold(first)
    first_mine = gathered(first)
    second_mine = gathered(second)
    second_halves = (second_mine, swap(second_mine, "src", 1))
    second_halves, _ = lax.optimization_barrier((second_halves, first_mine))
    other_in, other_out, diagonal_in, diagonal_out = adjoint(held, *second_halves)
    both = lambda here, there: (here.astype(F32) + swap(there, "rcv", 1).astype(F32)).astype(BF16)
    to_far = [both(other_out, diagonal_out), both(other_in, diagonal_in)]
    far_out, far_in = [swap(x, "rcv", 2) for x in to_far]
    first_theirs = swap(first_mine, "src", 1)
    first_theirs, _ = lax.optimization_barrier((first_theirs, to_far))
    mine_in, mine_out, *to_beside = adjoint(held, first_mine, first_theirs)
    beside_in, beside_out = [swap(x, "rcv", 1) for x in to_beside]

    edges = (mine_out.astype(F32) + beside_out.astype(F32) + far_out.astype(F32)).astype(BF16)
    top, bottom = exchange_edges(edges[:edge_cells], edges[edge_cells:])
    inside = jnp.stack([me > 0, me < tiles - 1]).astype(F32)
    inner, back_state = pl.pallas_call(
        back_inner_kernel,
        out_shape=(jax.ShapeDtypeStruct(by_half, F32), state),
        in_specs=[VMEM] * 8,
        out_specs=(VMEM, VMEM),
        scratch_shapes=[pltpu.VMEM((rows, SUB, lon), F32), pltpu.VMEM((cells, probe_local, BLK), F32)],
        compiler_params=params(),
        name="back_inner",
    )(flat, kappa, mine_in, beside_in, far_in, mine_out, beside_out, far_out)
    out = pl.pallas_call(
        back_outer_kernel,
        out_shape=jax.ShapeDtypeStruct((probe_local * rows, lon), F32),
        in_specs=[SMEM] + [VMEM] * 7,
        out_specs=HBM,
        scratch_shapes=[
            pltpu.VMEM(by_half, F32),
            pltpu.VMEM((halo_rows, SUB, lon), F32),
            pltpu.VMEM((2, edge_cells, probe_local, BLK), F32),
            pltpu.SemaphoreType.DMA((probe_local // SUB, halves)),
        ],
        compiler_params=params(),
        name="back_outer",
    )(inside, kappa, above, below, top, bottom, back_state, inner)
    return out.reshape(probe_local, rows, lon)


def solution(mesh):
    placed = (
        P("rcv", "src", None),
        P("src", None),
        P("src", "rcv", None, None, None),
        P("src", "rcv", None),
        P("src", "rcv", None),
        P("src", "rcv"),
        P("rcv"),
    )
    return jax.shard_map(
        per_device, mesh=mesh, in_specs=placed, out_specs=P("rcv", "src", None), check_vma=False
    )
```

```python
import jax
import jax.numpy as jnp
from jax import lax
from jax.experimental import pallas as pl
from jax.experimental.pallas import tpu as pltpu
from jax.sharding import PartitionSpec as P

BLK = 128
RB_LOC = 16
SMOOTH = 4
SUB = 8
PIECES = 16
GROUP = 96
FETCHES = 3
F32, BF16 = jnp.float32, jnp.bfloat16
VMEM = pl.BlockSpec(memory_space=pltpu.VMEM)
SMEM = pl.BlockSpec(memory_space=pltpu.SMEM)
HBM = pl.BlockSpec(memory_space=pltpu.HBM)


def in_hbm(x):
    return pltpu.with_memory_space_constraint(x, pltpu.HBM)


def params(mib=24):
    return pltpu.CompilerParams(vmem_limit_bytes=mib * 1024 * 1024)


def widen(probes_ref, wide):
    for h in range(wide.shape[0]):
        wide[h] = probes_ref[:, h * BLK : (h + 1) * BLK].astype(F32)


def one_row(wide, start, size, rows):
    at = pl.ds(start, size, stride=rows)
    return [wide[h, at, :] for h in range(wide.shape[0])]


def split_row(row):
    return [row[:, h * BLK : (h + 1) * BLK] for h in range(row.shape[1] // BLK)]


def around(north, row, south, lane):
    east = [pltpu.roll(x, 1, 1) for x in row]
    west = [pltpu.roll(x, BLK - 1, 1) for x in row]
    out = []
    for h, x in enumerate(row):
        left = jnp.where(lane > 0, east[h], east[h - 1] if h else 0.0)
        right = jnp.where(lane < BLK - 1, west[h], west[h + 1] if h + 1 < len(row) else 0.0)
        out.append(((north[h] + south[h]) + (left + right)) - 4.0 * x)
    return out


def edge_kernel(probes_hbm, kappa_hbm, north_ref, south_ref, probes_ref, kappa_ref, wide, arrived):
    fetches = [
        pltpu.make_async_copy(probes_hbm, probes_ref, arrived.at[0]),
        pltpu.make_async_copy(kappa_hbm, kappa_ref, arrived.at[1]),
    ]
    for fetch in fetches:
        fetch.start()
    for fetch in fetches:
        fetch.wait()
    rows, lon = kappa_ref.shape
    probe_local = probes_ref.shape[0] // rows
    widen(probes_ref, wide)
    place = lax.broadcasted_iota(jnp.int32, (PIECES, lon), 0)
    for out_ref, first in ((north_ref, 0), (south_ref, rows - SMOOTH)):
        pieces = jnp.zeros((PIECES, lon), F32)
        for r in range(SMOOTH):
            for h, part in enumerate(one_row(wide, first + r, probe_local, rows)):
                out_ref[r * probe_local : (r + 1) * probe_local, h * BLK : (h + 1) * BLK] = part.astype(BF16)
            whole = kappa_ref[first + r : first + r + 1, :]
            high = whole.astype(BF16).astype(F32)
            rest = whole - high
            middle = rest.astype(BF16).astype(F32)
            for i, piece in enumerate((high, middle, rest - middle)):
                pieces = jnp.where(place == i * SMOOTH + r, piece, pieces)
        out_ref[SMOOTH * probe_local :, :] = pieces.astype(BF16)


def kappa_rows(kappa_ref, above_ref, below_ref, probe_local):
    def halo(ref, r):
        pieces = ref[SMOOTH * probe_local :, :].astype(F32)
        high, middle, low = [pieces[i * SMOOTH + r : i * SMOOTH + r + 1] for i in range(3)]
        return high + middle + low

    rows = kappa_ref.shape[0]
    return (
        [halo(above_ref, r) for r in range(SMOOTH)]
        + [kappa_ref[r : r + 1, :] for r in range(rows)]
        + [halo(below_ref, r) for r in range(SMOOTH)]
    )


def put_row(ref, blk, at, row):
    for h, part in enumerate(row):
        ref[blk + h, at, :] = part


def smooth_step(f, coef, lane, r):
    lap = around(f[r - 1], f[r], f[r + 1], lane)
    return [x + coef[r, :, h * BLK : (h + 1) * BLK] * y for h, (x, y) in enumerate(zip(f[r], lap))]


def coefficients(coef, kappas):
    for r, k in kappas:
        coef[r] = jnp.broadcast_to(k, coef.shape[1:])


def lanes():
    return lax.broadcasted_iota(jnp.int32, (SUB, BLK), 1)


def keep_state(state_ref, step, f, at):
    rows = len(f)
    for side, first in ((0, step), (1, rows - 2 - step)):
        for i in range(2):
            for h, part in enumerate(f[first + i]):
                state_ref[side, step, i, at, h * BLK : (h + 1) * BLK] = part


def outer_rows(kappas):
    total, reach = len(kappas), 2 * SMOOTH + 1
    return [(r, k) for r, k in enumerate(kappas) if r < reach or r >= total - reach]


def smooth_inner_kernel(probes_ref, kappa_ref, field_ref, state_ref, wide, coef, result):
    rows, lon = kappa_ref.shape
    probe_local = probes_ref.shape[0] // rows
    halves = lon // BLK
    widen(probes_ref, wide)
    coefficients(coef, [(r, kappa_ref[r : r + 1, :]) for r in range(rows)])
    lane = lanes()

    @pl.loop(0, probe_local // SUB, unroll=2)
    def _(c):
        base = pl.multiple_of(c * SUB, SUB)
        at = pl.ds(base, SUB)
        f = [one_row(wide, base * rows + r, SUB, rows) for r in range(rows)]
        for step in range(SMOOTH):
            keep_state(state_ref, step, f, at)
            f = [smooth_step(f, coef, lane, r) if step < r < rows - 1 - step else f[r] for r in range(rows)]
        for r in range(SMOOTH, rows - SMOOTH):
            put_row(result, (r - SMOOTH) * halves, at, f[r])

    field_ref[...] = result[...].astype(BF16)


def side_rows(state_ref, side, step, mine, at):
    inner = [split_row(state_ref[side, step, i, at, :]) for i in range(2)]
    return mine + inner if side == 0 else inner + mine


def smooth_outer_kernel(kappa_ref, above_ref, below_ref, state_ref, field_ref, coef, halos, result):
    rows, lon = kappa_ref.shape
    probe_local = state_ref.shape[3]
    halves = lon // BLK
    for r in range(SMOOTH):
        halos[0, r] = above_ref[r * probe_local : (r + 1) * probe_local, :].astype(F32)
        halos[1, r] = below_ref[r * probe_local : (r + 1) * probe_local, :].astype(F32)
    coefficients(coef, outer_rows(kappa_rows(kappa_ref, above_ref, below_ref, probe_local)))
    lane = lanes()
    total = rows + 2 * SMOOTH

    @pl.loop(0, probe_local // SUB, unroll=2)
    def _(c):
        base = pl.multiple_of(c * SUB, SUB)
        at = pl.ds(base, SUB)
        for side in range(2):
            mine = [split_row(halos[side, r, at, :]) for r in range(SMOOTH)]
            for step in range(SMOOTH):
                f = side_rows(state_ref, side, step, mine, at)
                first = step if side == 0 else total - 6 - step
                rows_at = dict(enumerate(f, first))
                new = range(first + 1, first + 5)
                mine = [smooth_step(rows_at, coef, lane, r) for r in new]
            for r in range(SMOOTH):
                put_row(result, (side * SMOOTH + r) * halves, at, mine[r])

    field_ref[...] = result[...].astype(BF16)


def hold_kernel(blocks_ref, after_ref, held_ref, arrived):
    copy = pltpu.make_async_copy(blocks_ref, held_ref, arrived)
    copy.start()
    copy.wait()


def each_slot(slots, body):
    @pl.loop(0, slots // GROUP)
    def _(g):
        for i in range(GROUP):
            body(g * GROUP + i)


def forward_kernel(
    sources_hbm,
    receptors_hbm,
    count,
    place,
    blocks_ref,
    near_in,
    near_out,
    far_in,
    far_out,
    keep_ref,
    give_ref,
    turned,
    total,
    held,
    arrived,
    sources,
    receptors,
    listed,
):
    lists = [
        pltpu.make_async_copy(sources_hbm, sources, listed.at[0]),
        pltpu.make_async_copy(receptors_hbm, receptors, listed.at[1]),
    ]
    for fetch in lists:
        fetch.start()
    fetches = []
    size = held.shape[0] // FETCHES
    for g in range(FETCHES):
        at = pl.ds(g * size, size)
        fetches.append(pltpu.make_async_copy(blocks_ref.at[at], held.at[at], arrived.at[g]))
        fetches[g].start()
    total[...] = jnp.zeros_like(total)
    edge = near_out.shape[0] // 2
    for j in range(turned.shape[0]):
        if edge <= j < turned.shape[0] - edge:
            near, far = near_in[j - edge], far_in[j - edge]
        else:
            at = j if j < edge else j - near_in.shape[0]
            near, far = near_out[at], far_out[at]
        turned[j] = jnp.concatenate([near, far], axis=0).T

    spare = total.shape[0] - 1

    def slot(n):
        b = jnp.where(n < count[0], receptors[n], spare)
        total[b] += jnp.dot(held[n], turned[sources[n]], preferred_element_type=F32)

    for fetch in lists:
        fetch.wait()
    for g, fetch in enumerate(fetches):
        fetch.wait()
        for i in range(size):
            slot(g * size + i)
    half = keep_ref.shape[0]
    for out_ref, side in ((keep_ref, place[0]), (give_ref, 1 - place[0])):
        for b in range(half):
            out_ref[b] = total[side * half + b].T.astype(BF16)


def adjoint_kernel(
    sources, receptors, count, place, held, mine_ref, theirs_ref, near_in, near_out, far_in, far_out, weighted, total
):
    total[...] = jnp.zeros_like(total)
    pieces, share = mine_ref.shape[:2]
    for side_ref, side in ((mine_ref, place[0]), (theirs_ref, 1 - place[0])):
        for k in range(pieces):
            row = (side * pieces + lax.bitwise_xor(place[1], k)) * share
            weighted[pl.ds(pl.multiple_of(row, share), share), :] = side_ref[k]

    spare = total.shape[0] - 1
    pair = total.shape[1]

    def slot(n):
        j = jnp.where(n < count[0], sources[n], spare)
        entries = weighted[pl.ds(pl.multiple_of(receptors[n] * pair, pair), pair), :]
        total[j] += jnp.dot(entries, held[n], preferred_element_type=F32)

    each_slot(held.shape[0], slot)
    half = near_in.shape[1]
    edge = near_out.shape[0] // 2
    for at, in_ref, out_ref in ((pl.ds(0, half), near_in, near_out), (pl.ds(half, half), far_in, far_out)):
        out_ref[:edge] = total[:edge, at].astype(BF16)
        in_ref[...] = total[edge : spare - edge, at].astype(BF16)
        out_ref[edge:] = total[spare - edge : spare, at].astype(BF16)


def block_row(ref, first, at, halves):
    return [ref[first + h, at, :] for h in range(halves)]


def times_kappa(coef, f, r):
    return [coef[r, :, h * BLK : (h + 1) * BLK] * x for h, x in enumerate(f[r])]


def back_inner_kernel(
    probes_ref, kappa_ref, own_in, core_in, far_in, own_out, core_out, far_out, wide, state_ref, coef, terms
):
    rows, lon = kappa_ref.shape
    probe_local = probes_ref.shape[0] // rows
    halves = lon // BLK
    edge = own_out.shape[0] // 2
    widen(probes_ref, wide)
    inner = own_in[...].astype(F32) + core_in[...].astype(F32) + far_in[...].astype(F32)
    outer = own_out[...].astype(F32) + core_out[...].astype(F32) + far_out[...].astype(F32)
    terms[:edge] = outer[:edge]
    terms[edge : terms.shape[0] - edge] = inner
    terms[terms.shape[0] - edge :] = outer[edge:]
    lane = lanes()
    coefficients(coef, [(r, kappa_ref[r : r + 1, :]) for r in range(rows)])

    @pl.loop(0, probe_local // SUB, unroll=2)
    def _(c):
        base = pl.multiple_of(c * SUB, SUB)
        at = pl.ds(base, SUB)
        f = [block_row(terms, r * halves, at, halves) for r in range(rows)]
        for step in range(SMOOTH):
            keep_state(state_ref, step, f, at)
            g = {r: times_kappa(coef, f, r) for r in (step, step + 1)}
            new = list(f)
            for r in range(step + 1, rows - 1 - step):
                g[r + 1] = times_kappa(coef, f, r + 1)
                new[r] = [x + y for x, y in zip(f[r], around(g[r - 1], g[r], g[r + 1], lane))]
            f = new
        for r in range(SMOOTH, rows - SMOOTH):
            for h in range(halves):
                wide[h, pl.ds(base * rows + r, SUB, stride=rows), :] += f[r][h]


def back_outer_kernel(
    inside, kappa_ref, above_ref, below_ref, top_ref, bottom_ref, state_ref, done_ref, out_hbm, wide, coef, halos, sent
):
    rows, lon = kappa_ref.shape
    probe_local = state_ref.shape[3]
    halves = lon // BLK
    total = rows + 2 * SMOOTH
    halos[0] = top_ref[...].astype(F32)
    halos[1] = bottom_ref[...].astype(F32)
    lane = lanes()
    coefficients(coef, outer_rows(kappa_rows(kappa_ref, above_ref, below_ref, probe_local)))

    def sends(c):
        lines = pl.ds(pl.multiple_of(c * SUB * rows, SUB * rows), SUB * rows)
        return [
            pltpu.make_async_copy(wide.at[h, lines], out_hbm.at[lines, h * BLK : (h + 1) * BLK], sent.at[c, h])
            for h in range(halves)
        ]

    @pl.loop(0, probe_local // SUB, unroll=2)
    def _(c):
        base = pl.multiple_of(c * SUB, SUB)
        at = pl.ds(base, SUB)
        lines = pl.ds(pl.multiple_of(base * rows, SUB * rows), SUB * rows)
        wide[:, lines, :] = done_ref[:, lines, :]
        for side in range(2):
            mine = [block_row(halos.at[side], r * halves, at, halves) for r in range(SMOOTH)]
            for step in range(SMOOTH):
                first = step if side == 0 else total - 6 - step
                f = dict(enumerate(side_rows(state_ref, side, step, mine, at), first))
                g = {r: times_kappa(coef, f, r) for r in f}
                mine = []
                for r in range(first + 1, first + 5):
                    lap = around(g[r - 1], g[r], g[r + 1], lane)
                    if not SMOOTH <= r < total - SMOOTH:
                        lap = [x * inside[side] for x in lap]
                    mine.append([x + y for x, y in zip(f[r], lap)])
            for r in range(SMOOTH):
                row = r if side == 0 else rows - SMOOTH + r
                for h in range(halves):
                    wide[h, pl.ds(base * rows + row, SUB, stride=rows), :] += mine[r][h]
        for copy in sends(c):
            copy.start()

    for c in range(probe_local // SUB):
        for copy in sends(c):
            copy.wait()


def swap(x, axis, distance):
    size = lax.axis_size(axis)
    return lax.ppermute(x, axis, [(i, i ^ distance) for i in range(size)])


def far_first(size):
    return sorted(range(1, size), key=lambda k: -k.bit_length())


def exchange_edges(north, south):
    size = lax.axis_size("src")
    down = [(i, i + 1) for i in range(size - 1)]
    up = [(j, i) for i, j in down]
    return lax.ppermute(south, "src", down), lax.ppermute(north, "src", up)


def per_device(probes, kappa, footprint, block_source, block_receptor, block_count, obs_weight):
    probe_local, rows, lon = probes.shape
    halves = lon // BLK
    cells = rows * halves
    tiles = lax.axis_size("src")
    me = lax.axis_index("src")
    blocks = footprint.reshape(footprint.shape[2:])
    slots = blocks.shape[0]
    flat = probes.reshape(probe_local * rows, lon)
    pair = 2 * probe_local

    edge = jax.ShapeDtypeStruct((SMOOTH * probe_local + PIECES, lon), BF16)
    north, south, flat, kappa = pl.pallas_call(
        edge_kernel,
        out_shape=(edge, edge, jax.ShapeDtypeStruct(flat.shape, BF16), jax.ShapeDtypeStruct(kappa.shape, F32)),
        in_specs=[HBM, HBM],
        out_specs=(VMEM,) * 4,
        scratch_shapes=[
            pltpu.VMEM((halves, probe_local * rows, BLK), F32),
            pltpu.SemaphoreType.DMA((2,)),
        ],
        compiler_params=params(),
        name="edges",
    )(in_hbm(flat), in_hbm(kappa))
    above, below = exchange_edges(north, south)

    def hold(after):
        return pl.pallas_call(
            hold_kernel,
            out_shape=jax.ShapeDtypeStruct(blocks.shape, BF16),
            in_specs=[HBM, pl.BlockSpec(memory_space=pl.ANY)],
            out_specs=VMEM,
            scratch_shapes=[pltpu.SemaphoreType.DMA],
            compiler_params=params(),
            cost_estimate=pl.CostEstimate(flops=0, bytes_accessed=4 * slots * BLK * BLK, transcendentals=0),
            name="hold",
        )(in_hbm(blocks), after)

    edge_cells = SMOOTH * halves
    inner_part = jax.ShapeDtypeStruct((cells - 2 * edge_cells, probe_local, BLK), BF16)
    outer_part = jax.ShapeDtypeStruct((2 * edge_cells, probe_local, BLK), BF16)
    state = jax.ShapeDtypeStruct((2, SMOOTH, 2, probe_local, lon), F32)
    by_half = (halves, probe_local * rows, BLK)
    halo_rows = rows + 2 * SMOOTH
    own_in, smooth_state = pl.pallas_call(
        smooth_inner_kernel,
        out_shape=(inner_part, state),
        in_specs=[VMEM] * 2,
        out_specs=(VMEM, VMEM),
        scratch_shapes=[
            pltpu.VMEM(by_half, F32),
            pltpu.VMEM((rows, SUB, lon), F32),
            pltpu.VMEM(inner_part.shape, F32),
        ],
        compiler_params=params(),
        name="smooth_inner",
    )(flat, kappa)
    own_out = pl.pallas_call(
        smooth_outer_kernel,
        out_shape=outer_part,
        in_specs=[VMEM] * 4,
        out_specs=VMEM,
        scratch_shapes=[
            pltpu.VMEM((halo_rows, SUB, lon), F32),
            pltpu.VMEM((2, SMOOTH, probe_local, lon), F32),
            pltpu.VMEM(outer_part.shape, F32),
        ],
        compiler_params=params(),
        name="smooth_outer",
    )(kappa, above, below, smooth_state)

    side, row = me % 2, me // 2
    place = jnp.stack([side, row]).astype(jnp.int32)
    lists = (block_source.reshape(-1), block_receptor.reshape(-1))
    single = (block_count.reshape(-1), place)
    spread_over = tiles // 2
    share = RB_LOC * pair // tiles

    def over_slots(kernel, list_spec, lists, footprints_spec, footprints, operands, outs, scratch):
        return pl.pallas_call(
            kernel,
            out_shape=outs,
            in_specs=[list_spec, list_spec, SMEM, SMEM, footprints_spec] + [VMEM] * len(operands),
            out_specs=jax.tree.map(lambda _: VMEM, outs),
            scratch_shapes=scratch,
            compiler_params=params(),
            cost_estimate=pl.CostEstimate(
                flops=2 * slots * BLK * BLK * pair, bytes_accessed=2 * slots * BLK * BLK, transcendentals=0
            ),
            name=kernel.__name__,
        )(*lists, *single, footprints, *operands)

    def forward(*fields):
        half = jax.ShapeDtypeStruct((RB_LOC // 2, pair, BLK), BF16)
        return over_slots(
            forward_kernel,
            HBM,
            [in_hbm(x) for x in lists],
            HBM,
            in_hbm(blocks),
            fields,
            (half, half),
            [
                pltpu.VMEM((cells, BLK, pair), BF16),
                pltpu.VMEM((RB_LOC + 1, BLK, pair), F32),
                pltpu.VMEM(blocks.shape, BF16),
                pltpu.SemaphoreType.DMA((FETCHES,)),
                pltpu.SMEM((slots,), jnp.int32),
                pltpu.SMEM((slots,), jnp.int32),
                pltpu.SemaphoreType.DMA((2,)),
            ],
        )

    def adjoint(held, mine, theirs):
        return over_slots(
            adjoint_kernel,
            SMEM,
            lists,
            VMEM,
            held,
            (mine, theirs),
            (inner_part, outer_part) * 2,
            [pltpu.VMEM((RB_LOC * pair, BLK), BF16), pltpu.VMEM((cells + 1, pair, BLK), F32)],
        )

    first_row = (side * spread_over + row) * share
    held_blocks = max(share // pair, 1)
    weights = lax.dynamic_slice_in_dim(obs_weight.reshape(RB_LOC, 1, BLK), first_row // pair, held_blocks)
    weights = jnp.broadcast_to(weights, (held_blocks, share // held_blocks, BLK)).reshape(share, BLK)

    def summed(keep, give):
        got = swap(give, "src", 1)
        pairs = (keep.astype(F32) + got.astype(F32)).astype(BF16).reshape(spread_over, share, BLK)
        picked = lambda k: lax.dynamic_index_in_dim(pairs, lax.bitwise_xor(row, k), 0, False)
        total = picked(0).astype(F32)
        for k in far_first(spread_over):
            total = total + swap(picked(k), "src", 2 * k).astype(F32)
        return (weights * total).astype(BF16)

    def gathered(weighted):
        pieces = {k: swap(weighted, "src", 2 * k) for k in far_first(spread_over)}
        return jnp.stack([weighted] + [pieces[k] for k in range(1, spread_over)])

    def spread(weighted):
        mine = gathered(weighted)
        return mine, swap(mine, "src", 1)

    own = (own_in, own_out)
    other = [swap(x, "rcv", 2) for x in own]
    beside = [swap(x, "rcv", 1) for x in own]
    near_keep, near_give = forward(*own, *beside)
    other[1], near_give = lax.optimization_barrier((other[1], near_give))
    first = summed(near_keep, near_give)
    second = summed(*forward(*other, *[swap(x, "rcv", 1) for x in other]))

    held = hold(first)
    first_mine = gathered(first)
    second_mine = gathered(second)
    second_halves = (second_mine, swap(second_mine, "src", 1))
    second_halves, _ = lax.optimization_barrier((second_halves, first_mine))
    other_in, other_out, diagonal_in, diagonal_out = adjoint(held, *second_halves)
    both = lambda here, there: (here.astype(F32) + swap(there, "rcv", 1).astype(F32)).astype(BF16)
    to_far = [both(other_out, diagonal_out), both(other_in, diagonal_in)]
    far_out, far_in = [swap(x, "rcv", 2) for x in to_far]
    first_theirs = swap(first_mine, "src", 1)
    first_theirs, _ = lax.optimization_barrier((first_theirs, to_far))
    mine_in, mine_out, *to_beside = adjoint(held, first_mine, first_theirs)
    beside_in, beside_out = [swap(x, "rcv", 1) for x in to_beside]

    edges = (mine_out.astype(F32) + beside_out.astype(F32) + far_out.astype(F32)).astype(BF16)
    top, bottom = exchange_edges(edges[:edge_cells], edges[edge_cells:])
    inside = jnp.stack([me > 0, me < tiles - 1]).astype(F32)
    inner, back_state = pl.pallas_call(
        back_inner_kernel,
        out_shape=(jax.ShapeDtypeStruct(by_half, F32), state),
        in_specs=[VMEM] * 8,
        out_specs=(VMEM, VMEM),
        scratch_shapes=[pltpu.VMEM((rows, SUB, lon), F32), pltpu.VMEM((cells, probe_local, BLK), F32)],
        compiler_params=params(),
        name="back_inner",
    )(flat, kappa, mine_in, beside_in, far_in, mine_out, beside_out, far_out)
    out = pl.pallas_call(
        back_outer_kernel,
        out_shape=jax.ShapeDtypeStruct((probe_local * rows, lon), F32),
        in_specs=[SMEM] + [VMEM] * 7,
        out_specs=HBM,
        scratch_shapes=[
            pltpu.VMEM(by_half, F32),
            pltpu.VMEM((halo_rows, SUB, lon), F32),
            pltpu.VMEM((2, edge_cells, probe_local, BLK), F32),
            pltpu.SemaphoreType.DMA((probe_local // SUB, halves)),
        ],
        compiler_params=params(),
        name="back_outer",
    )(inside, kappa, above, below, top, bottom, back_state, inner)
    return out.reshape(probe_local, rows, lon)


def solution(mesh):
    placed = (
        P("rcv", "src", None),
        P("src", None),
        P("src", "rcv", None, None, None),
        P("src", "rcv", None),
        P("src", "rcv", None),
        P("src", "rcv"),
        P("rcv"),
    )
    return jax.shard_map(
        per_device, mesh=mesh, in_specs=placed, out_specs=P("rcv", "src", None), check_vma=False
    )
```

```python
import jax
import jax.numpy as jnp
from jax import lax
from jax.experimental import pallas as pl
from jax.experimental.pallas import tpu as pltpu
from jax.sharding import PartitionSpec as P

BLK = 128
RB_LOC = 16
SMOOTH = 4
SUB = 8
PIECES = 16
GROUP = 96
FETCHES = 3
F32, BF16 = jnp.float32, jnp.bfloat16
VMEM = pl.BlockSpec(memory_space=pltpu.VMEM)
SMEM = pl.BlockSpec(memory_space=pltpu.SMEM)
HBM = pl.BlockSpec(memory_space=pltpu.HBM)


def in_hbm(x):
    return pltpu.with_memory_space_constraint(x, pltpu.HBM)


def params(mib=24):
    return pltpu.CompilerParams(vmem_limit_bytes=mib * 1024 * 1024)


def widen(probes_ref, wide):
    for h in range(wide.shape[0]):
        wide[h] = probes_ref[:, h * BLK : (h + 1) * BLK].astype(F32)


def one_row(wide, start, size, rows):
    at = pl.ds(start, size, stride=rows)
    return [wide[h, at, :] for h in range(wide.shape[0])]


def split_row(row):
    return [row[:, h * BLK : (h + 1) * BLK] for h in range(row.shape[1] // BLK)]


def around(north, row, south, lane):
    east = [pltpu.roll(x, 1, 1) for x in row]
    west = [pltpu.roll(x, BLK - 1, 1) for x in row]
    out = []
    for h, x in enumerate(row):
        left = jnp.where(lane > 0, east[h], east[h - 1] if h else 0.0)
        right = jnp.where(lane < BLK - 1, west[h], west[h + 1] if h + 1 < len(row) else 0.0)
        out.append(((north[h] + south[h]) + (left + right)) - 4.0 * x)
    return out


def edge_kernel(probes_hbm, kappa_hbm, north_ref, south_ref, probes_ref, kappa_ref, wide, arrived):
    fetches = [
        pltpu.make_async_copy(probes_hbm, probes_ref, arrived.at[0]),
        pltpu.make_async_copy(kappa_hbm, kappa_ref, arrived.at[1]),
    ]
    for fetch in fetches:
        fetch.start()
    for fetch in fetches:
        fetch.wait()
    rows, lon = kappa_ref.shape
    probe_local = probes_ref.shape[0] // rows
    widen(probes_ref, wide)
    place = lax.broadcasted_iota(jnp.int32, (PIECES, lon), 0)
    for out_ref, first in ((north_ref, 0), (south_ref, rows - SMOOTH)):
        pieces = jnp.zeros((PIECES, lon), F32)
        for r in range(SMOOTH):
            for h, part in enumerate(one_row(wide, first + r, probe_local, rows)):
                out_ref[r * probe_local : (r + 1) * probe_local, h * BLK : (h + 1) * BLK] = part.astype(BF16)
            whole = kappa_ref[first + r : first + r + 1, :]
            high = whole.astype(BF16).astype(F32)
            rest = whole - high
            middle = rest.astype(BF16).astype(F32)
            for i, piece in enumerate((high, middle, rest - middle)):
                pieces = jnp.where(place == i * SMOOTH + r, piece, pieces)
        out_ref[SMOOTH * probe_local :, :] = pieces.astype(BF16)


def kappa_rows(kappa_ref, above_ref, below_ref, probe_local):
    def halo(ref, r):
        pieces = ref[SMOOTH * probe_local :, :].astype(F32)
        high, middle, low = [pieces[i * SMOOTH + r : i * SMOOTH + r + 1] for i in range(3)]
        return high + middle + low

    rows = kappa_ref.shape[0]
    return (
        [halo(above_ref, r) for r in range(SMOOTH)]
        + [kappa_ref[r : r + 1, :] for r in range(rows)]
        + [halo(below_ref, r) for r in range(SMOOTH)]
    )


def put_row(ref, blk, at, row):
    for h, part in enumerate(row):
        ref[blk + h, at, :] = part


def smooth_step(f, coef, lane, r):
    lap = around(f[r - 1], f[r], f[r + 1], lane)
    return [x + coef[r, :, h * BLK : (h + 1) * BLK] * y for h, (x, y) in enumerate(zip(f[r], lap))]


def coefficients(coef, kappas):
    for r, k in kappas:
        coef[r] = jnp.broadcast_to(k, coef.shape[1:])


def lanes():
    return lax.broadcasted_iota(jnp.int32, (SUB, BLK), 1)


def keep_state(state_ref, step, f, at):
    rows = len(f)
    for side, first in ((0, step), (1, rows - 2 - step)):
        for i in range(2):
            for h, part in enumerate(f[first + i]):
                state_ref[side, step, i, at, h * BLK : (h + 1) * BLK] = part


def outer_rows(kappas):
    total, reach = len(kappas), 2 * SMOOTH + 1
    return [(r, k) for r, k in enumerate(kappas) if r < reach or r >= total - reach]


def smooth_inner_kernel(probes_ref, kappa_ref, field_ref, state_ref, wide, coef, result):
    rows, lon = kappa_ref.shape
    probe_local = probes_ref.shape[0] // rows
    halves = lon // BLK
    widen(probes_ref, wide)
    coefficients(coef, [(r, kappa_ref[r : r + 1, :]) for r in range(rows)])
    lane = lanes()

    @pl.loop(0, probe_local // SUB, unroll=4)
    def _(c):
        base = pl.multiple_of(c * SUB, SUB)
        at = pl.ds(base, SUB)
        f = [one_row(wide, base * rows + r, SUB, rows) for r in range(rows)]
        for step in range(SMOOTH):
            keep_state(state_ref, step, f, at)
            f = [smooth_step(f, coef, lane, r) if step < r < rows - 1 - step else f[r] for r in range(rows)]
        for r in range(SMOOTH, rows - SMOOTH):
            put_row(result, (r - SMOOTH) * halves, at, f[r])

    field_ref[...] = result[...].astype(BF16)


def side_rows(state_ref, side, step, mine, at):
    inner = [split_row(state_ref[side, step, i, at, :]) for i in range(2)]
    return mine + inner if side == 0 else inner + mine


def smooth_outer_kernel(kappa_ref, above_ref, below_ref, state_ref, field_ref, coef, halos, result):
    rows, lon = kappa_ref.shape
    probe_local = state_ref.shape[3]
    halves = lon // BLK
    for r in range(SMOOTH):
        halos[0, r] = above_ref[r * probe_local : (r + 1) * probe_local, :].astype(F32)
        halos[1, r] = below_ref[r * probe_local : (r + 1) * probe_local, :].astype(F32)
    coefficients(coef, outer_rows(kappa_rows(kappa_ref, above_ref, below_ref, probe_local)))
    lane = lanes()
    total = rows + 2 * SMOOTH

    @pl.loop(0, probe_local // SUB, unroll=2)
    def _(c):
        base = pl.multiple_of(c * SUB, SUB)
        at = pl.ds(base, SUB)
        for side in range(2):
            mine = [split_row(halos[side, r, at, :]) for r in range(SMOOTH)]
            for step in range(SMOOTH):
                f = side_rows(state_ref, side, step, mine, at)
                first = step if side == 0 else total - 6 - step
                rows_at = dict(enumerate(f, first))
                new = range(first + 1, first + 5)
                mine = [smooth_step(rows_at, coef, lane, r) for r in new]
            for r in range(SMOOTH):
                put_row(result, (side * SMOOTH + r) * halves, at, mine[r])

    field_ref[...] = result[...].astype(BF16)


def hold_kernel(blocks_ref, after_ref, held_ref, arrived):
    copy = pltpu.make_async_copy(blocks_ref, held_ref, arrived)
    copy.start()
    copy.wait()


def each_slot(slots, body):
    @pl.loop(0, slots // GROUP)
    def _(g):
        for i in range(GROUP):
            body(g * GROUP + i)


def forward_kernel(
    sources_hbm,
    receptors_hbm,
    count,
    place,
    blocks_ref,
    near_in,
    near_out,
    far_in,
    far_out,
    keep_ref,
    give_ref,
    turned,
    total,
    held,
    arrived,
    sources,
    receptors,
    listed,
):
    lists = [
        pltpu.make_async_copy(sources_hbm, sources, listed.at[0]),
        pltpu.make_async_copy(receptors_hbm, receptors, listed.at[1]),
    ]
    for fetch in lists:
        fetch.start()
    fetches = []
    size = held.shape[0] // FETCHES
    for g in range(FETCHES):
        at = pl.ds(g * size, size)
        fetches.append(pltpu.make_async_copy(blocks_ref.at[at], held.at[at], arrived.at[g]))
        fetches[g].start()
    total[...] = jnp.zeros_like(total)
    edge = near_out.shape[0] // 2
    for j in range(turned.shape[0]):
        if edge <= j < turned.shape[0] - edge:
            near, far = near_in[j - edge], far_in[j - edge]
        else:
            at = j if j < edge else j - near_in.shape[0]
            near, far = near_out[at], far_out[at]
        turned[j] = jnp.concatenate([near, far], axis=0).T

    spare = total.shape[0] - 1

    def slot(n):
        b = jnp.where(n < count[0], receptors[n], spare)
        total[b] += jnp.dot(held[n], turned[sources[n]], preferred_element_type=F32)

    for fetch in lists:
        fetch.wait()
    for g, fetch in enumerate(fetches):
        fetch.wait()
        for i in range(size):
            slot(g * size + i)
    half = keep_ref.shape[0]
    for out_ref, side in ((keep_ref, place[0]), (give_ref, 1 - place[0])):
        for b in range(half):
            out_ref[b] = total[side * half + b].T.astype(BF16)


def adjoint_kernel(
    sources, receptors, count, place, held, mine_ref, theirs_ref, near_in, near_out, far_in, far_out, weighted, total
):
    total[...] = jnp.zeros_like(total)
    pieces, share = mine_ref.shape[:2]
    for side_ref, side in ((mine_ref, place[0]), (theirs_ref, 1 - place[0])):
        for k in range(pieces):
            row = (side * pieces + lax.bitwise_xor(place[1], k)) * share
            weighted[pl.ds(pl.multiple_of(row, share), share), :] = side_ref[k]

    spare = total.shape[0] - 1
    pair = total.shape[1]

    def slot(n):
        j = jnp.where(n < count[0], sources[n], spare)
        entries = weighted[pl.ds(pl.multiple_of(receptors[n] * pair, pair), pair), :]
        total[j] += jnp.dot(entries, held[n], preferred_element_type=F32)

    each_slot(held.shape[0], slot)
    half = near_in.shape[1]
    edge = near_out.shape[0] // 2
    for at, in_ref, out_ref in ((pl.ds(0, half), near_in, near_out), (pl.ds(half, half), far_in, far_out)):
        out_ref[:edge] = total[:edge, at].astype(BF16)
        in_ref[...] = total[edge : spare - edge, at].astype(BF16)
        out_ref[edge:] = total[spare - edge : spare, at].astype(BF16)


def block_row(ref, first, at, halves):
    return [ref[first + h, at, :] for h in range(halves)]


def times_kappa(coef, f, r):
    return [coef[r, :, h * BLK : (h + 1) * BLK] * x for h, x in enumerate(f[r])]


def back_inner_kernel(
    probes_ref, kappa_ref, own_in, core_in, far_in, own_out, core_out, far_out, wide, state_ref, coef, terms
):
    rows, lon = kappa_ref.shape
    probe_local = probes_ref.shape[0] // rows
    halves = lon // BLK
    edge = own_out.shape[0] // 2
    widen(probes_ref, wide)
    inner = own_in[...].astype(F32) + core_in[...].astype(F32) + far_in[...].astype(F32)
    outer = own_out[...].astype(F32) + core_out[...].astype(F32) + far_out[...].astype(F32)
    terms[:edge] = outer[:edge]
    terms[edge : terms.shape[0] - edge] = inner
    terms[terms.shape[0] - edge :] = outer[edge:]
    lane = lanes()
    coefficients(coef, [(r, kappa_ref[r : r + 1, :]) for r in range(rows)])

    @pl.loop(0, probe_local // SUB, unroll=4)
    def _(c):
        base = pl.multiple_of(c * SUB, SUB)
        at = pl.ds(base, SUB)
        f = [block_row(terms, r * halves, at, halves) for r in range(rows)]
        for step in range(SMOOTH):
            keep_state(state_ref, step, f, at)
            g = {r: times_kappa(coef, f, r) for r in (step, step + 1)}
            new = list(f)
            for r in range(step + 1, rows - 1 - step):
                g[r + 1] = times_kappa(coef, f, r + 1)
                new[r] = [x + y for x, y in zip(f[r], around(g[r - 1], g[r], g[r + 1], lane))]
            f = new
        for r in range(SMOOTH, rows - SMOOTH):
            for h in range(halves):
                wide[h, pl.ds(base * rows + r, SUB, stride=rows), :] += f[r][h]


def back_outer_kernel(
    inside, kappa_ref, above_ref, below_ref, top_ref, bottom_ref, state_ref, done_ref, out_hbm, wide, coef, halos, sent
):
    rows, lon = kappa_ref.shape
    probe_local = state_ref.shape[3]
    halves = lon // BLK
    total = rows + 2 * SMOOTH
    halos[0] = top_ref[...].astype(F32)
    halos[1] = bottom_ref[...].astype(F32)
    lane = lanes()
    coefficients(coef, outer_rows(kappa_rows(kappa_ref, above_ref, below_ref, probe_local)))

    def sends(c):
        lines = pl.ds(pl.multiple_of(c * SUB * rows, SUB * rows), SUB * rows)
        return [
            pltpu.make_async_copy(wide.at[h, lines], out_hbm.at[lines, h * BLK : (h + 1) * BLK], sent.at[c, h])
            for h in range(halves)
        ]

    @pl.loop(0, probe_local // SUB, unroll=2)
    def _(c):
        base = pl.multiple_of(c * SUB, SUB)
        at = pl.ds(base, SUB)
        lines = pl.ds(pl.multiple_of(base * rows, SUB * rows), SUB * rows)
        wide[:, lines, :] = done_ref[:, lines, :]
        for side in range(2):
            mine = [block_row(halos.at[side], r * halves, at, halves) for r in range(SMOOTH)]
            for step in range(SMOOTH):
                first = step if side == 0 else total - 6 - step
                f = dict(enumerate(side_rows(state_ref, side, step, mine, at), first))
                g = {r: times_kappa(coef, f, r) for r in f}
                mine = []
                for r in range(first + 1, first + 5):
                    lap = around(g[r - 1], g[r], g[r + 1], lane)
                    if not SMOOTH <= r < total - SMOOTH:
                        lap = [x * inside[side] for x in lap]
                    mine.append([x + y for x, y in zip(f[r], lap)])
            for r in range(SMOOTH):
                row = r if side == 0 else rows - SMOOTH + r
                for h in range(halves):
                    wide[h, pl.ds(base * rows + row, SUB, stride=rows), :] += mine[r][h]
        for copy in sends(c):
            copy.start()

    for c in range(probe_local // SUB):
        for copy in sends(c):
            copy.wait()


def swap(x, axis, distance):
    size = lax.axis_size(axis)
    return lax.ppermute(x, axis, [(i, i ^ distance) for i in range(size)])


def far_first(size):
    return sorted(range(1, size), key=lambda k: -k.bit_length())


def exchange_edges(north, south):
    size = lax.axis_size("src")
    down = [(i, i + 1) for i in range(size - 1)]
    up = [(j, i) for i, j in down]
    return lax.ppermute(south, "src", down), lax.ppermute(north, "src", up)


def per_device(probes, kappa, footprint, block_source, block_receptor, block_count, obs_weight):
    probe_local, rows, lon = probes.shape
    halves = lon // BLK
    cells = rows * halves
    tiles = lax.axis_size("src")
    me = lax.axis_index("src")
    blocks = footprint.reshape(footprint.shape[2:])
    slots = blocks.shape[0]
    flat = probes.reshape(probe_local * rows, lon)
    pair = 2 * probe_local

    edge = jax.ShapeDtypeStruct((SMOOTH * probe_local + PIECES, lon), BF16)
    north, south, flat, kappa = pl.pallas_call(
        edge_kernel,
        out_shape=(edge, edge, jax.ShapeDtypeStruct(flat.shape, BF16), jax.ShapeDtypeStruct(kappa.shape, F32)),
        in_specs=[HBM, HBM],
        out_specs=(VMEM,) * 4,
        scratch_shapes=[
            pltpu.VMEM((halves, probe_local * rows, BLK), F32),
            pltpu.SemaphoreType.DMA((2,)),
        ],
        compiler_params=params(),
        name="edges",
    )(in_hbm(flat), in_hbm(kappa))
    above, below = exchange_edges(north, south)

    def hold(after):
        return pl.pallas_call(
            hold_kernel,
            out_shape=jax.ShapeDtypeStruct(blocks.shape, BF16),
            in_specs=[HBM, pl.BlockSpec(memory_space=pl.ANY)],
            out_specs=VMEM,
            scratch_shapes=[pltpu.SemaphoreType.DMA],
            compiler_params=params(),
            cost_estimate=pl.CostEstimate(flops=0, bytes_accessed=4 * slots * BLK * BLK, transcendentals=0),
            name="hold",
        )(in_hbm(blocks), after)

    edge_cells = SMOOTH * halves
    inner_part = jax.ShapeDtypeStruct((cells - 2 * edge_cells, probe_local, BLK), BF16)
    outer_part = jax.ShapeDtypeStruct((2 * edge_cells, probe_local, BLK), BF16)
    state = jax.ShapeDtypeStruct((2, SMOOTH, 2, probe_local, lon), F32)
    by_half = (halves, probe_local * rows, BLK)
    halo_rows = rows + 2 * SMOOTH
    own_in, smooth_state = pl.pallas_call(
        smooth_inner_kernel,
        out_shape=(inner_part, state),
        in_specs=[VMEM] * 2,
        out_specs=(VMEM, VMEM),
        scratch_shapes=[
            pltpu.VMEM(by_half, F32),
            pltpu.VMEM((rows, SUB, lon), F32),
            pltpu.VMEM(inner_part.shape, F32),
        ],
        compiler_params=params(),
        name="smooth_inner",
    )(flat, kappa)
    own_out = pl.pallas_call(
        smooth_outer_kernel,
        out_shape=outer_part,
        in_specs=[VMEM] * 4,
        out_specs=VMEM,
        scratch_shapes=[
            pltpu.VMEM((halo_rows, SUB, lon), F32),
            pltpu.VMEM((2, SMOOTH, probe_local, lon), F32),
            pltpu.VMEM(outer_part.shape, F32),
        ],
        compiler_params=params(),
        name="smooth_outer",
    )(kappa, above, below, smooth_state)

    side, row = me % 2, me // 2
    place = jnp.stack([side, row]).astype(jnp.int32)
    lists = (block_source.reshape(-1), block_receptor.reshape(-1))
    single = (block_count.reshape(-1), place)
    spread_over = tiles // 2
    share = RB_LOC * pair // tiles

    def over_slots(kernel, list_spec, lists, footprints_spec, footprints, operands, outs, scratch):
        return pl.pallas_call(
            kernel,
            out_shape=outs,
            in_specs=[list_spec, list_spec, SMEM, SMEM, footprints_spec] + [VMEM] * len(operands),
            out_specs=jax.tree.map(lambda _: VMEM, outs),
            scratch_shapes=scratch,
            compiler_params=params(),
            cost_estimate=pl.CostEstimate(
                flops=2 * slots * BLK * BLK * pair, bytes_accessed=2 * slots * BLK * BLK, transcendentals=0
            ),
            name=kernel.__name__,
        )(*lists, *single, footprints, *operands)

    def forward(*fields):
        half = jax.ShapeDtypeStruct((RB_LOC // 2, pair, BLK), BF16)
        return over_slots(
            forward_kernel,
            HBM,
            [in_hbm(x) for x in lists],
            HBM,
            in_hbm(blocks),
            fields,
            (half, half),
            [
                pltpu.VMEM((cells, BLK, pair), BF16),
                pltpu.VMEM((RB_LOC + 1, BLK, pair), F32),
                pltpu.VMEM(blocks.shape, BF16),
                pltpu.SemaphoreType.DMA((FETCHES,)),
                pltpu.SMEM((slots,), jnp.int32),
                pltpu.SMEM((slots,), jnp.int32),
                pltpu.SemaphoreType.DMA((2,)),
            ],
        )

    def adjoint(held, mine, theirs):
        return over_slots(
            adjoint_kernel,
            SMEM,
            lists,
            VMEM,
            held,
            (mine, theirs),
            (inner_part, outer_part) * 2,
            [pltpu.VMEM((RB_LOC * pair, BLK), BF16), pltpu.VMEM((cells + 1, pair, BLK), F32)],
        )

    first_row = (side * spread_over + row) * share
    held_blocks = max(share // pair, 1)
    weights = lax.dynamic_slice_in_dim(obs_weight.reshape(RB_LOC, 1, BLK), first_row // pair, held_blocks)
    weights = jnp.broadcast_to(weights, (held_blocks, share // held_blocks, BLK)).reshape(share, BLK)

    def summed(keep, give):
        got = swap(give, "src", 1)
        pairs = (keep.astype(F32) + got.astype(F32)).astype(BF16).reshape(spread_over, share, BLK)
        picked = lambda k: lax.dynamic_index_in_dim(pairs, lax.bitwise_xor(row, k), 0, False)
        total = picked(0).astype(F32)
        for k in far_first(spread_over):
            total = total + swap(picked(k), "src", 2 * k).astype(F32)
        return (weights * total).astype(BF16)

    def gathered(weighted):
        pieces = {k: swap(weighted, "src", 2 * k) for k in far_first(spread_over)}
        return jnp.stack([weighted] + [pieces[k] for k in range(1, spread_over)])

    def spread(weighted):
        mine = gathered(weighted)
        return mine, swap(mine, "src", 1)

    own = (own_in, own_out)
    other = [swap(x, "rcv", 2) for x in own]
    beside = [swap(x, "rcv", 1) for x in own]
    near_keep, near_give = forward(*own, *beside)
    other[1], near_give = lax.optimization_barrier((other[1], near_give))
    first = summed(near_keep, near_give)
    second = summed(*forward(*other, *[swap(x, "rcv", 1) for x in other]))

    held = hold(first)
    first_mine = gathered(first)
    second_mine = gathered(second)
    second_halves = (second_mine, swap(second_mine, "src", 1))
    second_halves, _ = lax.optimization_barrier((second_halves, first_mine))
    other_in, other_out, diagonal_in, diagonal_out = adjoint(held, *second_halves)
    both = lambda here, there: (here.astype(F32) + swap(there, "rcv", 1).astype(F32)).astype(BF16)
    to_far = [both(other_out, diagonal_out), both(other_in, diagonal_in)]
    far_out, far_in = [swap(x, "rcv", 2) for x in to_far]
    first_theirs = swap(first_mine, "src", 1)
    first_theirs, _ = lax.optimization_barrier((first_theirs, to_far))
    mine_in, mine_out, *to_beside = adjoint(held, first_mine, first_theirs)
    beside_in, beside_out = [swap(x, "rcv", 1) for x in to_beside]

    edges = (mine_out.astype(F32) + beside_out.astype(F32) + far_out.astype(F32)).astype(BF16)
    top, bottom = exchange_edges(edges[:edge_cells], edges[edge_cells:])
    inside = jnp.stack([me > 0, me < tiles - 1]).astype(F32)
    inner, back_state = pl.pallas_call(
        back_inner_kernel,
        out_shape=(jax.ShapeDtypeStruct(by_half, F32), state),
        in_specs=[VMEM] * 8,
        out_specs=(VMEM, VMEM),
        scratch_shapes=[pltpu.VMEM((rows, SUB, lon), F32), pltpu.VMEM((cells, probe_local, BLK), F32)],
        compiler_params=params(),
        name="back_inner",
    )(flat, kappa, mine_in, beside_in, far_in, mine_out, beside_out, far_out)
    out = pl.pallas_call(
        back_outer_kernel,
        out_shape=jax.ShapeDtypeStruct((probe_local * rows, lon), F32),
        in_specs=[SMEM] + [VMEM] * 7,
        out_specs=HBM,
        scratch_shapes=[
            pltpu.VMEM(by_half, F32),
            pltpu.VMEM((halo_rows, SUB, lon), F32),
            pltpu.VMEM((2, edge_cells, probe_local, BLK), F32),
            pltpu.SemaphoreType.DMA((probe_local // SUB, halves)),
        ],
        compiler_params=params(),
        name="back_outer",
    )(inside, kappa, above, below, top, bottom, back_state, inner)
    return out.reshape(probe_local, rows, lon)


def solution(mesh):
    placed = (
        P("rcv", "src", None),
        P("src", None),
        P("src", "rcv", None, None, None),
        P("src", "rcv", None),
        P("src", "rcv", None),
        P("src", "rcv"),
        P("rcv"),
    )
    return jax.shard_map(
        per_device, mesh=mesh, in_specs=placed, out_specs=P("rcv", "src", None), check_vma=False
    )
```
